512 devices in a mesh: gx: 8 (over y), gy: 16 (over z, x_lo), gz: 4 (over x_hi, core).
Axes of the slice: x: 4 (x_hi: 2, x_lo: 2; x = x_hi * 2 + x_lo), y: 8, z: 8, core: 2. Of those that a mesh axis runs over, the one named last changes fastest.
Arguments:
- pops: float32 [27, 16, 128, 1024], P(None, 'gz', 'gy', 'gx')
- solid: int32 [16, 128, 1024], P('gz', 'gy', 'gx'), may hold values from 0 to 1, as said below
- profile_table: float32 [8, 16], P(None, 'gz'), as said below
- profile_index: int32 [128], P('gy'), may hold values from 0 to 7
Outputs:
- updated: float32 [27, 16, 128, 1024], P(None, 'gz', 'gy', 'gx')
The draws below stay inside these ranges and needn't reach their ends.
Inputs may be any that keep to these rules, and one draw needn't show every extreme that they name: `solid`: buildings are vertical columns on footprints of 4 x 4 cells aligned to multiples of 4; every cell with z index 15 is 0. `profile_table`: every profile's speeds lie in a band of positive values.
All inputs are finite; a program needn't handle non-finite values.
Results may differ from the reference program's by a relative error of at most 0.0003.
Values sent between devices are 32-bit elements; how exact they have to be, the bound alone decides.
A program may use at most 64 MiB of HBM per device.

```python
import jax
import jax.numpy as jnp
import numpy as np
from jax import lax

STEPS = 2
PROF = 8
NX = 1024
NY = 128
NZ = 16
SPONGE = 32


def lattice_drawn():
    velocity = np.array([[cx, cy, cz] for cz in (-1, 0, 1) for cy in (-1, 0, 1) for cx in (-1, 0, 1)])
    lengths_sq = (velocity * velocity).sum(1)
    weights = np.array([8.0 / 27.0, 2.0 / 27.0, 1.0 / 54.0, 1.0 / 216.0])[lengths_sq]
    return (velocity, weights)


def draw_pops(key, part):
    velocity, weights = lattice_drawn()
    keys = jax.random.split(jax.random.fold_in(key, 11), 6)
    shape = (NZ, NY, NX)
    height = (jnp.arange(NZ, dtype=jnp.float32)[:, None, None] + 0.5) / NZ
    rough = jax.random.uniform(keys[0], shape, jnp.float32, 0.5, 1.5)
    noise = jnp.clip(jax.random.normal(keys[4], (27,) + shape, jnp.float32), -2.0, 2.0)
    amplitude = jnp.exp(jax.random.uniform(keys[5], shape, jnp.float32, jnp.log(0.1), jnp.log(0.4)))
    speed_x = 0.12 * (0.2 + 0.8 * height) * rough
    speed_y = 0.04 * jnp.clip(jax.random.normal(keys[1], shape, jnp.float32), -3.0, 3.0)
    speed_z = 0.03 * jnp.clip(jax.random.normal(keys[2], shape, jnp.float32), -3.0, 3.0)
    density = 1.0 + 0.03 * jnp.clip(jax.random.normal(keys[3], shape, jnp.float32), -3.0, 3.0)
    comp_x = jnp.asarray(velocity[:, 0], jnp.float32).reshape(27, 1, 1, 1)
    comp_y = jnp.asarray(velocity[:, 1], jnp.float32).reshape(27, 1, 1, 1)
    comp_z = jnp.asarray(velocity[:, 2], jnp.float32).reshape(27, 1, 1, 1)
    factor = jnp.asarray(weights, jnp.float32).reshape(27, 1, 1, 1)
    along = comp_x * speed_x + comp_y * speed_y + comp_z * speed_z
    square = speed_x * speed_x + speed_y * speed_y + speed_z * speed_z
    balance = factor * density * (1.0 + 3.0 * along + 4.5 * along * along - 1.5 * square)
    return (balance + factor * amplitude[None] * noise).astype(jnp.float32)


def draw_solid(key, part):
    heights = jax.random.randint(jax.random.fold_in(key, 23), (NY // 4, NX // 4), -(NZ - 1), NZ)
    heights = jnp.maximum(heights, 0)
    heights = heights.at[0, 0].set(NZ - 1)
    heights = heights.at[0, 1].set(0)
    heights = jnp.repeat(jnp.repeat(heights, 4, axis=0), 4, axis=1)
    level = jnp.arange(NZ, dtype=jnp.int32)[:, None, None]
    return (level < heights[None]).astype(jnp.int32)


def draw_profile_table(key, part):
    keys = jax.random.split(jax.random.fold_in(key, 37), 3)
    height = (jnp.arange(NZ, dtype=jnp.float32)[None, :] + 0.5) / NZ
    exponent = jnp.exp(jax.random.uniform(keys[0], (PROF, 1), jnp.float32, jnp.log(0.1), jnp.log(0.5)))
    scale = jax.random.uniform(keys[1], (PROF, 1), jnp.float32, 0.1, 0.18)
    rough = jax.random.uniform(keys[2], (PROF, NZ), jnp.float32, 0.7, 1.3)
    return (scale * (0.1 + height ** exponent) * rough).astype(jnp.float32)


def with_ends(values, own_key, smallest, high):
    dims = values.shape
    index_at = [jax.random.randint(jax.random.fold_in(own_key, axis), (), 0, dims[axis]) for axis in range(len(dims))]
    values = values.at[tuple(index_at)].set(smallest)
    longest = dims.index(max(dims))
    index_at[longest] = (index_at[longest] + 1) % dims[longest]
    return values.at[tuple(index_at)].set(high)


def setup_inputs(seed: int = 0) -> dict:
    seeds = jax.random.split(jax.random.key(seed), 5)
    pops = draw_pops(jax.random.fold_in(seeds[4], 71), 0)
    solid = draw_solid(jax.random.fold_in(seeds[4], 71), 0)
    profile_table = draw_profile_table(jax.random.fold_in(seeds[4], 71), 0)
    profile_index = with_ends(jax.random.randint(seeds[3], (NY,), 0, PROF), jax.random.fold_in(seeds[3], 1), 0, PROF - 1).astype(jnp.int32)
    return dict(pops=pops, solid=solid, profile_table=profile_table, profile_index=profile_index)


tau_base = 0.52
smag_const = 0.17

def lattice():
    velocity = np.array([[cx, cy, cz] for cz in (-1, 0, 1) for cy in (-1, 0, 1) for cx in (-1, 0, 1)])
    lengths_sq = (velocity * velocity).sum(1)
    weights = np.array([8.0 / 27.0, 2.0 / 27.0, 1.0 / 54.0, 1.0 / 216.0])[lengths_sq]
    return (velocity, weights)

def mirror_of(number):
    velocity, weights = lattice()
    cx, cy, cz = velocity[number]
    return int((1 - cz) * 9 + (cy + 1) * 3 + (cx + 1))

def equilibrium(density, speed_x, speed_y, speed_z):
    velocity, weights = lattice()
    comp_x = jnp.asarray(velocity[:, 0], jnp.float32).reshape(27, 1, 1, 1)
    comp_y = jnp.asarray(velocity[:, 1], jnp.float32).reshape(27, 1, 1, 1)
    comp_z = jnp.asarray(velocity[:, 2], jnp.float32).reshape(27, 1, 1, 1)
    factor = jnp.asarray(weights, jnp.float32).reshape(27, 1, 1, 1)
    along = comp_x * speed_x + comp_y * speed_y + comp_z * speed_z
    square = speed_x * speed_x + speed_y * speed_y + speed_z * speed_z
    return factor * density * (1.0 + 3.0 * along + 4.5 * along * along - 1.5 * square)

def collide(pops):
    velocity, weights = lattice()
    first_table = np.concatenate([np.ones((27, 1)), velocity], axis=1)
    moments = jnp.einsum('qm,qzyx->mzyx', jnp.asarray(first_table, jnp.float32), pops, precision=lax.Precision.HIGHEST)
    density = moments[0]
    speed_x = moments[1] / density
    speed_y = moments[2] / density
    speed_z = moments[3] / density
    nonequil = pops - equilibrium(density, speed_x, speed_y, speed_z)
    pair_table = np.stack([velocity[:, 0] * velocity[:, 0], velocity[:, 1] * velocity[:, 1], velocity[:, 2] * velocity[:, 2], velocity[:, 0] * velocity[:, 1], velocity[:, 0] * velocity[:, 2], velocity[:, 1] * velocity[:, 2]], axis=1)
    stress = jnp.einsum('qm,qzyx->mzyx', jnp.asarray(pair_table, jnp.float32), nonequil, precision=lax.Precision.HIGHEST)
    strain_sq = stress[0] ** 2 + stress[1] ** 2 + stress[2] ** 2 + 2.0 * (stress[3] ** 2 + stress[4] ** 2 + stress[5] ** 2)
    magnitude = jnp.sqrt(2.0 * strain_sq)
    relax = 0.5 * (tau_base + jnp.sqrt(tau_base * tau_base + 18.0 * math_root_two() * smag_const * smag_const * magnitude / density))
    return (pops - nonequil / relax, density)

def math_root_two():
    return 1.4142135623730951

def reference(pops, solid, profile_table, profile_index):
    velocity, weights = lattice()
    onehot = (profile_index[:, None] == jnp.arange(PROF, dtype=jnp.int32)[None, :]).astype(jnp.float32)
    target = jnp.einsum('yp,pz->zy', onehot, profile_table, precision=lax.Precision.HIGHEST)[:, :, None]
    sponge = (jnp.arange(NX, dtype=jnp.int32) < SPONGE)[None, None, None, :]
    height = jnp.arange(NZ, dtype=jnp.int32)[:, None, None]
    fluid = (solid == 0)[None]
    rest = jnp.asarray(weights, jnp.float32).reshape(27, 1, 1, 1)
    walls = jnp.pad(solid, ((1, 1), (0, 0), (0, 0)))
    for step in range(STEPS):
        post, density = collide(pops)
        zeros = jnp.zeros_like(density)
        pinned = equilibrium(density, target + zeros, zeros, zeros)
        post = jnp.where(sponge, pinned, post)
        padded = jnp.pad(post, ((0, 0), (1, 1), (0, 0), (0, 0)))
        pieces = []
        for number in range(27):
            cx, cy, cz = [int(value) for value in velocity[number]]
            source = jnp.roll(padded[number], (cy, cx), axis=(1, 2))[1 - cz:1 - cz + NZ]
            blocked = jnp.roll(walls, (cy, cx), axis=(1, 2))[1 - cz:1 - cz + NZ] == 1
            bounce = post[26 - number]
            mirror = jnp.roll(post[mirror_of(number)], (cy, cx), axis=(1, 2))
            value = jnp.where(blocked, bounce, source)
            value = jnp.where(height - cz < 0, bounce, value)
            value = jnp.where(height - cz > NZ - 1, mirror, value)
            pieces.append(value)
        pops = jnp.where(fluid, jnp.stack(pieces), rest)
    return pops
```

```python
import functools

import jax
import jax.numpy as jnp
from jax import lax
from jax.experimental import pallas as pl
from jax.experimental.pallas import tpu as pltpu
from jax.sharding import PartitionSpec as P

SPONGE = 32
TAU = 0.52
SMAG = 0.17
ROOT_TWO = 1.4142135623730951
WEIGHT = (8.0 / 27.0, 2.0 / 27.0, 1.0 / 54.0, 1.0 / 216.0)
F32 = jnp.float32
SIDES = (-1, 0, 1)
VELOCITY = [(cx, cy, cz) for cz in SIDES for cy in SIDES for cx in SIDES]
DIRS = [(dx, dy, dz) for dx in SIDES for dy in SIDES for dz in SIDES if (dx, dy, dz) != (0, 0, 0)]
Z = 4
Y = 8
X = 128


def num(cx, cy, cz):
    return 9 * (cz + 1) + 3 * (cy + 1) + cx + 1


def weight(q):
    return WEIGHT[sum(c * c for c in VELOCITY[q])]


def lane_of(cy, cz, z):
    return 9 * z + 3 * (cz + 1) + cy + 1


def y_groups():
    table, row = {(1, Z - 1): 0, (-1, 0): 4}, 8
    for z in range(Z):
        for cz in SIDES:
            if (cz, z) not in table:
                table[cz, z] = row
                row += 3
    solid = {Z - 1: 3, 0: 7}
    for z in range(1, Z - 1):
        solid[z] = row
        row += 1
    assert row == 40
    return table, solid


Y_ROW, Y_SOLID = y_groups()


def total(values):
    values = list(values)
    while len(values) > 1:
        values = [a + b for a, b in zip(values[::2], values[1::2])] + (
            [values[-1]] if len(values) % 2 else []
        )
    return values[0]


def collide(f, target, sponge):
    s, d, e = {}, {}, {}
    for cz in SIDES:
        for cy in SIDES:
            lo, mid, hi = (f[num(cx, cy, cz)] for cx in SIDES)
            e[cy, cz] = hi + lo
            s[cy, cz] = e[cy, cz] + mid
            d[cy, cz] = hi - lo
    sy = {cy: total(s[cy, cz] for cz in SIDES) for cy in SIDES}
    sz = {cz: total(s[cy, cz] for cy in SIDES) for cz in SIDES}
    dy = {cy: total(d[cy, cz] for cz in SIDES) for cy in SIDES}
    dz = {cz: total(d[cy, cz] for cy in SIDES) for cz in (-1, 1)}
    rho = sy[-1] + sy[0] + sy[1]
    mx, my, mz = dy[-1] + dy[0] + dy[1], sy[1] - sy[-1], sz[1] - sz[-1]
    inv = 1.0 / rho
    ux, uy, uz = mx * inv, my * inv, mz * inv
    third = rho * (1.0 / 3.0)
    pxx = total(e.values()) - third - mx * ux
    pyy = (sy[1] + sy[-1]) - third - my * uy
    pzz = (sz[1] + sz[-1]) - third - mz * uz
    pxy = dy[1] - dy[-1] - mx * uy
    pxz = dz[1] - dz[-1] - mx * uz
    pyz = (s[1, 1] - s[-1, 1]) - (s[1, -1] - s[-1, -1]) - my * uz
    strain = (pxx * pxx + pyy * pyy + pzz * pzz) + 2.0 * (pxy * pxy + pxz * pxz + pyz * pyz)
    size = jnp.sqrt(2.0 * strain)
    tau = 0.5 * (TAU + jnp.sqrt(TAU * TAU + (18.0 * ROOT_TWO * SMAG * SMAG) * size * inv))
    omega = 1.0 / tau
    keep = 1.0 - omega
    base = 1.0 - 1.5 * (ux * ux + uy * uy + uz * uz)
    gain = omega * rho
    gains = [gain * w for w in WEIGHT]
    wx, wy, wz = 3.0 * ux, 3.0 * uy, 3.0 * uz
    t2 = 1.5 * target * target
    t3 = 3.0 * target
    pin_along = {0: 1.0 - t2, 1: 1.0 + t3 + 2.0 * t2, -1: 1.0 - t3 + 2.0 * t2}
    rhos = [rho * w for w in WEIGHT]
    pins = {}
    for cx in SIDES:
        for rest in range(3):
            pins[cx, rest] = rhos[cx * cx + rest] * pin_along[cx]
    post = [None] * 27
    for q in range(13, 27):
        cx, cy, cz = VELOCITY[q]
        kind = cx * cx + cy * cy + cz * cz
        if q == 13:
            post[q] = f[q] * keep + gains[0] * base
        else:
            along = None
            for c, w in ((cx, wx), (cy, wy), (cz, wz)):
                if c:
                    along = (w if c > 0 else -w) if along is None else (along + w if c > 0 else along - w)
            even = base + 0.5 * along * along
            post[q] = f[q] * keep + gains[kind] * (even + along)
            post[26 - q] = f[26 - q] * keep + gains[kind] * (even - along)
    for q in range(27):
        cx, cy, cz = VELOCITY[q]
        post[q] = jnp.where(sponge, pins[cx, cy * cy + cz * cz], post[q])
    return post


def kernel(
    sizes, pops_hbm, solid_ref, target_ref, out_ref,
    fin, post, xpk, ypk, zr, yr, er, xr, masks,
    in_sem, send_sem, recv_sem,
):
    nx, ny, nz = sizes
    gx, gy, gz = lax.axis_index("gx"), lax.axis_index("gy"), lax.axis_index("gz")
    at_top, at_bottom = gz == nz - 1, gz == 0

    def neighbour(d):
        dx, dy, dz = d
        px = gx if dx == 0 else lax.rem(gx + (dx + nx), nx)
        py = gy if dy == 0 else lax.rem(gy + (dy + ny), ny)
        return px, py, gz + dz

    def along_z(dz, body):
        if dz == 0:
            body()
        else:
            pl.when(jnp.logical_not(at_top if dz > 0 else at_bottom))(body)

    barrier = pltpu.get_barrier_semaphore()
    for dz in SIDES:
        def greet(dz=dz):
            for d in DIRS:
                if d[2] == dz:
                    pl.semaphore_signal(
                        barrier, inc=1, device_id=neighbour(d), device_id_type=pl.DeviceIdType.MESH
                    )
        along_z(dz, greet)

    loads = []
    for z in (0, 3, 1, 2):
        copy = pltpu.make_async_copy(pops_hbm.at[:, z], fin.at[z], in_sem.at[z])
        copy.start()
        loads.append((z, copy))

    row = lax.broadcasted_iota(jnp.int32, (Y, X), 0)
    lane = lax.broadcasted_iota(jnp.int32, (Y, X), 1)
    edge_row = {1: row == 0, -1: row == Y - 1}
    edge_lane = {1: lane == 0, -1: lane == X - 1}
    sponge = (lane < SPONGE - gx * X)
    top_mask = jnp.broadcast_to(at_top, (Y, X)) if False else (row * 0 + gz) == nz - 1
    bottom_mask = (row * 0 + gz) == 0

    def dst_of(step, d):
        dx, dy, dz = d
        if dx:
            return xr.at[step, DIRS.index(d)]
        if dy == 0:
            return zr.at[step, (dz + 1) // 2, pl.ds(0, (10 - step) * Y)]
        if dz == 0:
            return yr.at[step, (dy + 1) // 2]
        return er.at[step, dy + 1 + (dz + 1) // 2]

    def src_of(step, d):
        dx, dy, dz = d
        if dx:
            return xpk.at[step, (dx + 1) // 2]
        if dy == 0:
            if dz > 0:
                return post.at[step, Z - 1, pl.ds(19 * Y, (10 - step) * Y)]
            return post.at[step, 0, pl.ds(step * Y, (10 - step) * Y)]
        if dz == 0:
            return ypk.at[step, (dy + 1) // 2]
        return ypk.at[step, (dy + 1) // 2, pl.ds(0, Y)]

    def message(step, d):
        i = DIRS.index(d)
        return pltpu.make_async_remote_copy(
            src_ref=src_of(step, d), dst_ref=dst_of(step, d),
            send_sem=send_sem.at[step, i], recv_sem=recv_sem.at[step, i],
            device_id=neighbour(d), device_id_type=pl.DeviceIdType.MESH,
        )

    def each(step, chosen, what):
        for dz in SIDES:
            dirs = [d for d in chosen if d[2] == dz]
            if dirs:
                def body(dirs=dirs):
                    for d in dirs:
                        getattr(message(step, d), what)()
                along_z(-dz if what == "wait_recv" else dz, body)

    z_dirs = [d for d in DIRS if d[0] == 0 and d[1] == 0]
    y_dirs = [d for d in DIRS if d[0] == 0 and d[1] != 0]
    x_dirs = [d for d in DIRS if d[0] != 0]

    def put(step, z, values):
        for q in range(27):
            post[step, z, (q + 1) * Y:(q + 2) * Y, :] = values[q]

    def tile(step, z, q):
        return post[step, z, (q + 1) * Y:(q + 2) * Y, :]

    def pack(step, packed, z, values, solid):
        for side in (-1, 1):
            acc = packed[side]
            for cy in SIDES:
                for cz in SIDES:
                    col = lane_of(cy, cz, z)
                    shift = (col - (X - 1 if side > 0 else 0)) % X
                    acc = jnp.where(lane == col, pltpu.roll(values[num(side, cy, cz)], shift, 1), acc)
            if step == 0:
                col = 36 + z
                shift = (col - (X - 1 if side > 0 else 0)) % X
                acc = jnp.where(lane == col, pltpu.roll(solid, shift, 1), acc)
            packed[side] = acc
        for side in (-1, 1):
            own = Y - 1 if side > 0 else 0
            for cz in SIDES:
                start = Y_ROW[cz, z]
                first = (num(-1, side, cz) + 1) * Y + own
                ypk[step, (side + 1) // 2, start:start + 3, :] = post[
                    step, z, pl.ds(first, 3, stride=Y), :
                ]
            if step == 0:
                at = Y_SOLID[z]
                ypk[step, (side + 1) // 2, at:at + 1, :] = post[step, z, own:own + 1, :]

    def exchange(step, plane):
        packed = {side: jnp.zeros((Y, X), F32) for side in (-1, 1)}
        for z in (0, 3, 1, 2):
            values = collide(plane(z), target_ref[z], sponge)
            put(step, z, values)
            solid = None
            if step == 0:
                solid = solid_ref[z].astype(F32)
                post[step, z, 0:Y, :] = solid
                post[step, z, 28 * Y:29 * Y, :] = solid
            pack(step, packed, z, values, solid)
            if z == 3:
                if step == 0:
                    pl.semaphore_wait(barrier, jnp.where(at_top | at_bottom, 17, 26))
                each(step, z_dirs, "start")
        for side in (-1, 1):
            xpk[step, (side + 1) // 2] = packed[side]
        each(step, y_dirs, "start")
        each(step, x_dirs, "start")
        each(step, x_dirs, "wait_recv")
        each(step, y_dirs, "wait_recv")
        each(step, z_dirs, "wait_recv")

    def columns(step):
        result = {}
        for cx in (-1, 1):
            for dz in (0, -1, 1):
                near = xr[step, DIRS.index((cx, 0, dz))]
                for cy in SIDES:
                    got = near
                    if cy:
                        far = xr[step, DIRS.index((cx, cy, dz))]
                        got = pltpu.roll(jnp.where(edge_row[-cy], far, near), cy % Y, 0)
                    if dz == -1:
                        mirrored = pltpu.roll(result[cx, cy, 0], X - 33, 1)
                        got = jnp.where(top_mask, mirrored, got)
                    result[cx, cy, dz] = got
        return result

    def shift(value, cx, cy, line, column, col):
        if cy:
            value = jnp.where(edge_row[cy], line(), pltpu.roll(value, cy % Y, 0))
        if cx:
            spot = 0 if cx > 0 else X - 1
            value = jnp.where(
                edge_lane[cx], pltpu.roll(column, (spot - col) % X, 1), pltpu.roll(value, cx % X, 1)
            )
        return value

    def y_line(step, cy, at):
        return jnp.broadcast_to(yr[step, (cy + 1) // 2, at:at + 1, :], (Y, X))

    def e_line(step, cy, dz, at):
        return jnp.broadcast_to(er[step, cy + 1 + (dz + 1) // 2, at:at + 1, :], (Y, X))

    def build_masks(cols):
        for cx in SIDES:
            for cy in SIDES:
                for z in range(-1, Z + 1):
                    if 0 <= z < Z:
                        dz, col, value = 0, 36 + z, post[0, z, 0:Y, :]
                        line = lambda: y_line(0, cy, Y_SOLID[z])
                    elif z < 0:
                        dz, col, value = 1, 36 + Z - 1, zr[0, 1, 9 * Y:10 * Y, :]
                        line = lambda: e_line(0, cy, 1, 3)
                    else:
                        dz, col, value = -1, 36, zr[0, 0, 0:Y, :]
                        line = lambda: e_line(0, cy, -1, 7)
                    value = shift(value, cx, cy, line, cols.get((cx, cy, dz)), col)
                    if z < 0:
                        value = jnp.where(bottom_mask, 1.0, value)
                    if z == Z:
                        value = jnp.where(top_mask, 0.0, value)
                    masks[(3 * (cy + 1) + cx + 1) * (Z + 2) + z + 1] = value

    def stream(step, z, cols):
        own = post[0, z, 0:Y, :] > 0.5
        result = []
        for q in range(27):
            cx, cy, cz = VELOCITY[q]
            at = z - cz
            if 0 <= at < Z:
                value = tile(step, at, q)
                dz, col = 0, lane_of(cy, cz, at)
                line = lambda: y_line(step, cy, Y_ROW[cz, at] + cx + 1)
            elif at < 0:
                value = zr[step, 1, (q - 18) * Y:(q - 17) * Y, :]
                dz, col = 1, lane_of(cy, cz, Z - 1)
                line = lambda: e_line(step, cy, 1, cx + 1)
            else:
                first = (q + 1 - step) * Y
                value = jnp.where(top_mask, tile(step, Z - 1, num(cx, cy, 1)), zr[step, 0, first:first + Y, :])
                dz, col = -1, lane_of(cy, cz, 0)
                line = lambda: jnp.where(
                    top_mask, y_line(step, cy, Y_ROW[1, Z - 1] + cx + 1), e_line(step, cy, -1, 4 + cx + 1)
                )
            value = shift(value, cx, cy, line, cols.get((cx, cy, dz)), col)
            if q != 13:
                blocked = masks[(3 * (cy + 1) + cx + 1) * (Z + 2) + at + 1] > 0.5
                value = jnp.where(blocked, tile(step, z, 26 - q), value)
            result.append(jnp.where(own, weight(q), value))
        return result

    def first_plane(z):
        dict(loads)[z].wait()
        return [fin[z, q] for q in range(27)]

    exchange(0, first_plane)
    cols = columns(0)
    build_masks(cols)
    exchange(1, lambda z: stream(0, z, cols))
    cols = columns(1)
    for z in range(Z):
        values = stream(1, z, cols)
        for q in range(27):
            out_ref[q, z] = values[q]
    for step in range(2):
        for dirs in (z_dirs, y_dirs, x_dirs):
            each(step, dirs, "wait_send")


def shards(mesh_shape, pops, solid, profile_table, profile_index):
    profiles = profile_table.shape[0]
    onehot = profile_index[:, None] == jnp.arange(profiles, dtype=jnp.int32)[None, :]
    target = jnp.sum(
        jnp.where(onehot[None, :, :], profile_table.T[:, None, :], 0.0), axis=2
    )
    target = jnp.broadcast_to(target[:, :, None], (Z, Y, X))
    vmem = pl.BlockSpec(memory_space=pltpu.VMEM)
    return pl.pallas_call(
        functools.partial(kernel, mesh_shape),
        out_shape=jax.ShapeDtypeStruct(pops.shape, F32),
        in_specs=[pl.BlockSpec(memory_space=pl.ANY), vmem, vmem],
        out_specs=vmem,
        scratch_shapes=[
            pltpu.VMEM((Z, 27, Y, X), F32),
            pltpu.VMEM((2, Z, 29 * Y, X), F32),
            pltpu.VMEM((2, 2, Y, X), F32),
            pltpu.VMEM((2, 2, 40, X), F32),
            pltpu.VMEM((2, 2, 10 * Y, X), F32),
            pltpu.VMEM((2, 2, 40, X), F32),
            pltpu.VMEM((2, 4, Y, X), F32),
            pltpu.VMEM((2, 26, Y, X), F32),
            pltpu.VMEM((9 * (Z + 2), Y, X), F32),
            pltpu.SemaphoreType.DMA((Z,)),
            pltpu.SemaphoreType.DMA((2, 26)),
            pltpu.SemaphoreType.DMA((2, 26)),
        ],
        compiler_params=pltpu.CompilerParams(
            collective_id=0, has_side_effects=True, vmem_limit_bytes=32 * 1024 * 1024
        ),
    )(pops, solid, target)


def solution(mesh):
    sizes = tuple(mesh.shape[axis] for axis in ("gx", "gy", "gz"))
    return jax.shard_map(
        functools.partial(shards, sizes),
        mesh=mesh,
        in_specs=(P(None, "gz", "gy", "gx"), P("gz", "gy", "gx"), P(None, "gz"), P("gy")),
        out_specs=P(None, "gz", "gy", "gx"),
        check_vma=False,
    )
```

```python
import functools

import jax
import jax.numpy as jnp
from jax import lax
from jax.experimental import pallas as pl
from jax.experimental.pallas import tpu as pltpu
from jax.sharding import PartitionSpec as P

SPONGE = 32
TAU = 0.52
SMAG = 0.17
ROOT_TWO = 1.4142135623730951
WEIGHT = (8.0 / 27.0, 2.0 / 27.0, 1.0 / 54.0, 1.0 / 216.0)
F32 = jnp.float32
SIDES = (-1, 0, 1)
VELOCITY = [(cx, cy, cz) for cz in SIDES for cy in SIDES for cx in SIDES]
DIRS = [(dx, dy, dz) for dx in SIDES for dy in SIDES for dz in SIDES if (dx, dy, dz) != (0, 0, 0)]
Z = 4
Y = 8
X = 128


def num(cx, cy, cz):
    return 9 * (cz + 1) + 3 * (cy + 1) + cx + 1


def weight(q):
    return WEIGHT[sum(c * c for c in VELOCITY[q])]


def lane_of(cy, cz, z):
    return 9 * z + 3 * (cz + 1) + cy + 1


def y_groups():
    table, row = {(1, Z - 1): 0, (-1, 0): 4}, 8
    for z in range(Z):
        for cz in SIDES:
            if (cz, z) not in table:
                table[cz, z] = row
                row += 3
    solid = {Z - 1: 3, 0: 7}
    for z in range(1, Z - 1):
        solid[z] = row
        row += 1
    assert row == 40
    return table, solid


Y_ROW, Y_SOLID = y_groups()


def total(values):
    values = list(values)
    while len(values) > 1:
        values = [a + b for a, b in zip(values[::2], values[1::2])] + (
            [values[-1]] if len(values) % 2 else []
        )
    return values[0]


def collide(f, target, sponge):
    s, d, e = {}, {}, {}
    for cz in SIDES:
        for cy in SIDES:
            lo, mid, hi = (f[num(cx, cy, cz)] for cx in SIDES)
            e[cy, cz] = hi + lo
            s[cy, cz] = e[cy, cz] + mid
            d[cy, cz] = hi - lo
    sy = {cy: total(s[cy, cz] for cz in SIDES) for cy in SIDES}
    sz = {cz: total(s[cy, cz] for cy in SIDES) for cz in SIDES}
    dy = {cy: total(d[cy, cz] for cz in SIDES) for cy in SIDES}
    dz = {cz: total(d[cy, cz] for cy in SIDES) for cz in (-1, 1)}
    rho = sy[-1] + sy[0] + sy[1]
    mx, my, mz = dy[-1] + dy[0] + dy[1], sy[1] - sy[-1], sz[1] - sz[-1]
    inv = 1.0 / rho
    ux, uy, uz = mx * inv, my * inv, mz * inv
    third = rho * (1.0 / 3.0)
    pxx = total(e.values()) - third - mx * ux
    pyy = (sy[1] + sy[-1]) - third - my * uy
    pzz = (sz[1] + sz[-1]) - third - mz * uz
    pxy = dy[1] - dy[-1] - mx * uy
    pxz = dz[1] - dz[-1] - mx * uz
    pyz = (s[1, 1] - s[-1, 1]) - (s[1, -1] - s[-1, -1]) - my * uz
    strain = (pxx * pxx + pyy * pyy + pzz * pzz) + 2.0 * (pxy * pxy + pxz * pxz + pyz * pyz)
    size = jnp.sqrt(2.0 * strain)
    tau = 0.5 * (TAU + jnp.sqrt(TAU * TAU + (18.0 * ROOT_TWO * SMAG * SMAG) * size * inv))
    omega = 1.0 / tau
    keep = 1.0 - omega
    base = 1.0 - 1.5 * (ux * ux + uy * uy + uz * uz)
    gain = omega * rho
    gains = [gain * w for w in WEIGHT]
    wx, wy, wz = 3.0 * ux, 3.0 * uy, 3.0 * uz
    t2 = 1.5 * target * target
    t3 = 3.0 * target
    pin_along = {0: 1.0 - t2, 1: 1.0 + t3 + 2.0 * t2, -1: 1.0 - t3 + 2.0 * t2}
    rhos = [rho * w for w in WEIGHT]
    pins = {}
    for cx in SIDES:
        for rest in range(3):
            pins[cx, rest] = rhos[cx * cx + rest] * pin_along[cx]
    post = [None] * 27
    for q in range(13, 27):
        cx, cy, cz = VELOCITY[q]
        kind = cx * cx + cy * cy + cz * cz
        if q == 13:
            post[q] = f[q] * keep + gains[0] * base
        else:
            along = None
            for c, w in ((cx, wx), (cy, wy), (cz, wz)):
                if c:
                    along = (w if c > 0 else -w) if along is None else (along + w if c > 0 else along - w)
            even = base + 0.5 * along * along
            post[q] = f[q] * keep + gains[kind] * (even + along)
            post[26 - q] = f[26 - q] * keep + gains[kind] * (even - along)
    for q in range(27):
        cx, cy, cz = VELOCITY[q]
        post[q] = jnp.where(sponge, pins[cx, cy * cy + cz * cz], post[q])
    return post


def kernel(
    sizes, pops_hbm, solid_hbm, table_hbm, index_hbm, out_ref,
    fin, solid_ref, table_ref, index_ref, target_ref, post, xpk, ypk, zr, yr, er, xr, masks,
    in_sem, send_sem, recv_sem,
):
    nx, ny, nz = sizes
    gx, gy, gz = lax.axis_index("gx"), lax.axis_index("gy"), lax.axis_index("gz")
    at_top, at_bottom = gz == nz - 1, gz == 0

    def neighbour(d):
        dx, dy, dz = d
        px = gx if dx == 0 else lax.rem(gx + (dx + nx), nx)
        py = gy if dy == 0 else lax.rem(gy + (dy + ny), ny)
        return px, py, gz + dz

    def along_z(dz, body):
        if dz == 0:
            body()
        else:
            pl.when(jnp.logical_not(at_top if dz > 0 else at_bottom))(body)

    barrier = pltpu.get_barrier_semaphore()
    for dz in SIDES:
        def greet(dz=dz):
            for d in DIRS:
                if d[2] == dz:
                    pl.semaphore_signal(
                        barrier, inc=1, device_id=neighbour(d), device_id_type=pl.DeviceIdType.MESH
                    )
        along_z(dz, greet)

    small = [
        pltpu.make_async_copy(src, dst, in_sem.at[Z + i])
        for i, (src, dst) in enumerate(
            ((index_hbm, index_ref), (table_hbm, table_ref), (solid_hbm, solid_ref))
        )
    ]
    for copy in small:
        copy.start()
    loads = {}
    for z in (0, 3, 1, 2):
        loads[z] = pltpu.make_async_copy(pops_hbm.at[:, z], fin.at[z], in_sem.at[z])
        loads[z].start()

    row = lax.broadcasted_iota(jnp.int32, (Y, X), 0)
    lane = lax.broadcasted_iota(jnp.int32, (Y, X), 1)
    edge_row = {1: row == 0, -1: row == Y - 1}
    edge_lane = {1: lane == 0, -1: lane == X - 1}
    sponge = (lane < SPONGE - gx * X)
    top_mask = (row * 0 + gz) == nz - 1
    bottom_mask = (row * 0 + gz) == 0

    def dst_of(step, d):
        dx, dy, dz = d
        if dx:
            return xr.at[step, DIRS.index(d)]
        if dy == 0:
            return zr.at[step, (dz + 1) // 2, pl.ds(0, (10 - step) * Y)]
        if dz == 0:
            return yr.at[step, (dy + 1) // 2]
        return er.at[step, dy + 1 + (dz + 1) // 2]

    def src_of(step, d):
        dx, dy, dz = d
        if dx:
            return xpk.at[step, (dx + 1) // 2]
        if dy == 0:
            if dz > 0:
                return post.at[step, Z - 1, pl.ds(19 * Y, (10 - step) * Y)]
            return post.at[step, 0, pl.ds(step * Y, (10 - step) * Y)]
        if dz == 0:
            return ypk.at[step, (dy + 1) // 2]
        return ypk.at[step, (dy + 1) // 2, pl.ds(0, Y)]

    def message(step, d):
        i = DIRS.index(d)
        return pltpu.make_async_remote_copy(
            src_ref=src_of(step, d), dst_ref=dst_of(step, d),
            send_sem=send_sem.at[step, i], recv_sem=recv_sem.at[step, i],
            device_id=neighbour(d), device_id_type=pl.DeviceIdType.MESH,
        )

    def each(step, chosen, what):
        for dz in SIDES:
            dirs = [d for d in chosen if d[2] == dz]
            if dirs:
                def body(dirs=dirs):
                    for d in dirs:
                        getattr(message(step, d), what)()
                along_z(-dz if what == "wait_recv" else dz, body)

    z_dirs = [d for d in DIRS if d[0] == 0 and d[1] == 0]
    y_dirs = [d for d in DIRS if d[0] == 0 and d[1] != 0]
    x_dirs = [d for d in DIRS if d[0] != 0]

    def put(step, z, values):
        for q in range(27):
            post[step, z, (q + 1) * Y:(q + 2) * Y, :] = values[q]

    def tile(step, z, q):
        return post[step, z, (q + 1) * Y:(q + 2) * Y, :]

    def pack(step, packed, z, values, solid):
        for side in (-1, 1):
            acc = packed[side]
            for cy in SIDES:
                for cz in SIDES:
                    col = lane_of(cy, cz, z)
                    shift = (col - (X - 1 if side > 0 else 0)) % X
                    acc = jnp.where(lane == col, pltpu.roll(values[num(side, cy, cz)], shift, 1), acc)
            if step == 0:
                col = 36 + z
                shift = (col - (X - 1 if side > 0 else 0)) % X
                acc = jnp.where(lane == col, pltpu.roll(solid, shift, 1), acc)
            packed[side] = acc
        for side in (-1, 1):
            own = Y - 1 if side > 0 else 0
            for cz in SIDES:
                start = Y_ROW[cz, z]
                first = (num(-1, side, cz) + 1) * Y + own
                ypk[step, (side + 1) // 2, start:start + 3, :] = post[
                    step, z, pl.ds(first, 3, stride=Y), :
                ]
            if step == 0:
                at = Y_SOLID[z]
                ypk[step, (side + 1) // 2, at:at + 1, :] = post[step, z, own:own + 1, :]

    def exchange(step, plane):
        packed = {side: jnp.zeros((Y, X), F32) for side in (-1, 1)}
        for z in (0, 3, 1, 2):
            values = collide(plane(z), target_ref[z], sponge)
            put(step, z, values)
            solid = None
            if step == 0:
                solid = solid_ref[z].astype(F32)
                post[step, z, 0:Y, :] = solid
                post[step, z, 28 * Y:29 * Y, :] = solid
            pack(step, packed, z, values, solid)
            if z == 3:
                if step == 0:
                    pl.semaphore_wait(barrier, jnp.where(at_top | at_bottom, 17, 26))
                each(step, z_dirs, "start")
        for side in (-1, 1):
            xpk[step, (side + 1) // 2] = packed[side]
        each(step, y_dirs, "start")
        each(step, x_dirs, "start")
        each(step, x_dirs, "wait_recv")
        each(step, y_dirs, "wait_recv")
        each(step, z_dirs, "wait_recv")

    def columns(step):
        result = {}
        for cx in (-1, 1):
            for dz in (0, -1, 1):
                near = xr[step, DIRS.index((cx, 0, dz))]
                for cy in SIDES:
                    got = near
                    if cy:
                        far = xr[step, DIRS.index((cx, cy, dz))]
                        got = pltpu.roll(jnp.where(edge_row[-cy], far, near), cy % Y, 0)
                    if dz == -1:
                        mirrored = pltpu.roll(result[cx, cy, 0], X - 33, 1)
                        got = jnp.where(top_mask, mirrored, got)
                    result[cx, cy, dz] = got
        return result

    def shift(value, cx, cy, line, column, col):
        if cy:
            value = jnp.where(edge_row[cy], line(), pltpu.roll(value, cy % Y, 0))
        if cx:
            spot = 0 if cx > 0 else X - 1
            value = jnp.where(
                edge_lane[cx], pltpu.roll(column, (spot - col) % X, 1), pltpu.roll(value, cx % X, 1)
            )
        return value

    def y_line(step, cy, at):
        return jnp.broadcast_to(yr[step, (cy + 1) // 2, at:at + 1, :], (Y, X))

    def e_line(step, cy, dz, at):
        return jnp.broadcast_to(er[step, cy + 1 + (dz + 1) // 2, at:at + 1, :], (Y, X))

    def build_masks(cols):
        for cx in SIDES:
            for cy in SIDES:
                for z in range(-1, Z + 1):
                    if 0 <= z < Z:
                        dz, col, value = 0, 36 + z, post[0, z, 0:Y, :]
                        line = lambda: y_line(0, cy, Y_SOLID[z])
                    elif z < 0:
                        dz, col, value = 1, 36 + Z - 1, zr[0, 1, 9 * Y:10 * Y, :]
                        line = lambda: e_line(0, cy, 1, 3)
                    else:
                        dz, col, value = -1, 36, zr[0, 0, 0:Y, :]
                        line = lambda: e_line(0, cy, -1, 7)
                    value = shift(value, cx, cy, line, cols.get((cx, cy, dz)), col)
                    if z < 0:
                        value = jnp.where(bottom_mask, 1.0, value)
                    if z == Z:
                        value = jnp.where(top_mask, 0.0, value)
                    masks[(3 * (cy + 1) + cx + 1) * (Z + 2) + z + 1] = value

    def stream(step, z, cols):
        own = post[0, z, 0:Y, :] > 0.5
        result = []
        for q in range(27):
            cx, cy, cz = VELOCITY[q]
            at = z - cz
            if 0 <= at < Z:
                value = tile(step, at, q)
                dz, col = 0, lane_of(cy, cz, at)
                line = lambda: y_line(step, cy, Y_ROW[cz, at] + cx + 1)
            elif at < 0:
                value = zr[step, 1, (q - 18) * Y:(q - 17) * Y, :]
                dz, col = 1, lane_of(cy, cz, Z - 1)
                line = lambda: e_line(step, cy, 1, cx + 1)
            else:
                first = (q + 1 - step) * Y
                value = jnp.where(top_mask, tile(step, Z - 1, num(cx, cy, 1)), zr[step, 0, first:first + Y, :])
                dz, col = -1, lane_of(cy, cz, 0)
                line = lambda: jnp.where(
                    top_mask, y_line(step, cy, Y_ROW[1, Z - 1] + cx + 1), e_line(step, cy, -1, 4 + cx + 1)
                )
            value = shift(value, cx, cy, line, cols.get((cx, cy, dz)), col)
            if q != 13:
                blocked = masks[(3 * (cy + 1) + cx + 1) * (Z + 2) + at + 1] > 0.5
                value = jnp.where(blocked, tile(step, z, 26 - q), value)
            result.append(jnp.where(own, weight(q), value))
        return result

    def first_plane(z):
        loads[z].wait()
        return [fin[z, q] for q in range(27)]

    for copy in small:
        copy.wait()
    which = row * 0
    for y in range(Y):
        which = jnp.where(row == y, index_ref[y], which)
    for z in range(Z):
        target = jnp.zeros((Y, X), F32)
        for p in range(table_ref.shape[1]):
            entry = jnp.broadcast_to(table_ref[z:z + 1, p:p + 1], (Y, X))
            target = jnp.where(which == p, entry, target)
        target_ref[z] = target
    exchange(0, first_plane)
    cols = columns(0)
    build_masks(cols)
    exchange(1, lambda z: stream(0, z, cols))
    cols = columns(1)
    for z in range(Z):
        values = stream(1, z, cols)
        for q in range(27):
            out_ref[q, z] = values[q]
    for step in range(2):
        for dirs in (z_dirs, y_dirs, x_dirs):
            each(step, dirs, "wait_send")


def shards(mesh_shape, pops, solid, profile_table, profile_index):
    vmem = pl.BlockSpec(memory_space=pltpu.VMEM)
    return pl.pallas_call(
        functools.partial(kernel, mesh_shape),
        out_shape=jax.ShapeDtypeStruct(pops.shape, F32),
        in_specs=[pl.BlockSpec(memory_space=pltpu.HBM)] * 4,
        out_specs=vmem,
        scratch_shapes=[
            pltpu.VMEM((Z, 27, Y, X), F32),
            pltpu.VMEM((Z, Y, X), jnp.int32),
            pltpu.VMEM((Z, profile_table.shape[0]), F32),
            pltpu.SMEM((Y,), jnp.int32),
            pltpu.VMEM((Z, Y, X), F32),
            pltpu.VMEM((2, Z, 29 * Y, X), F32),
            pltpu.VMEM((2, 2, Y, X), F32),
            pltpu.VMEM((2, 2, 40, X), F32),
            pltpu.VMEM((2, 2, 10 * Y, X), F32),
            pltpu.VMEM((2, 2, 40, X), F32),
            pltpu.VMEM((2, 4, Y, X), F32),
            pltpu.VMEM((2, 26, Y, X), F32),
            pltpu.VMEM((9 * (Z + 2), Y, X), F32),
            pltpu.SemaphoreType.DMA((Z + 3,)),
            pltpu.SemaphoreType.DMA((2, 26)),
            pltpu.SemaphoreType.DMA((2, 26)),
        ],
        compiler_params=pltpu.CompilerParams(
            collective_id=0, has_side_effects=True, vmem_limit_bytes=32 * 1024 * 1024
        ),
    )(*[pltpu.with_memory_space_constraint(a, pltpu.HBM) for a in (pops, solid, profile_table.T, profile_index)])


def solution(mesh):
    sizes = tuple(mesh.shape[axis] for axis in ("gx", "gy", "gz"))
    return jax.shard_map(
        functools.partial(shards, sizes),
        mesh=mesh,
        in_specs=(P(None, "gz", "gy", "gx"), P("gz", "gy", "gx"), P(None, "gz"), P("gy")),
        out_specs=P(None, "gz", "gy", "gx"),
        check_vma=False,
    )
```

```python
import functools

import jax
import jax.numpy as jnp
from jax import lax
from jax.experimental import pallas as pl
from jax.experimental.pallas import tpu as pltpu
from jax.sharding import PartitionSpec as P

SPONGE = 32
TAU = 0.52
SMAG = 0.17
ROOT_TWO = 1.4142135623730951
WEIGHT = (8.0 / 27.0, 2.0 / 27.0, 1.0 / 54.0, 1.0 / 216.0)
F32 = jnp.float32
SIDES = (-1, 0, 1)
VELOCITY = [(cx, cy, cz) for cz in SIDES for cy in SIDES for cx in SIDES]
DIRS = [(dx, dy, dz) for dx in SIDES for dy in SIDES for dz in SIDES if (dx, dy, dz) != (0, 0, 0)]
FAR_FIRST = sorted(DIRS, key=lambda d: (d[0] == 0, d[1] == 0, d[2] == 0))
Z = 4
Y = 8
X = 128


def num(cx, cy, cz):
    return 9 * (cz + 1) + 3 * (cy + 1) + cx + 1


def weight(q):
    return WEIGHT[sum(c * c for c in VELOCITY[q])]


def lane_of(cy, cz, z):
    return 9 * z + 3 * (cz + 1) + cy + 1


def y_groups():
    table, row = {(1, Z - 1): 0, (-1, 0): 4}, 8
    for z in range(Z):
        for cz in SIDES:
            if (cz, z) not in table:
                table[cz, z] = row
                row += 3
    solid = {Z - 1: 3, 0: 7}
    for z in range(1, Z - 1):
        solid[z] = row
        row += 1
    assert row == 40
    return table, solid


Y_ROW, Y_SOLID = y_groups()


def total(values):
    values = list(values)
    while len(values) > 1:
        values = [a + b for a, b in zip(values[::2], values[1::2])] + (
            [values[-1]] if len(values) % 2 else []
        )
    return values[0]


def collide(f, target, sponge):
    s, d, e = {}, {}, {}
    for cz in SIDES:
        for cy in SIDES:
            lo, mid, hi = (f[num(cx, cy, cz)] for cx in SIDES)
            e[cy, cz] = hi + lo
            s[cy, cz] = e[cy, cz] + mid
            d[cy, cz] = hi - lo
    sy = {cy: total(s[cy, cz] for cz in SIDES) for cy in SIDES}
    sz = {cz: total(s[cy, cz] for cy in SIDES) for cz in SIDES}
    dy = {cy: total(d[cy, cz] for cz in SIDES) for cy in SIDES}
    dz = {cz: total(d[cy, cz] for cy in SIDES) for cz in (-1, 1)}
    rho = sy[-1] + sy[0] + sy[1]
    mx, my, mz = dy[-1] + dy[0] + dy[1], sy[1] - sy[-1], sz[1] - sz[-1]
    inv = 1.0 / rho
    ux, uy, uz = mx * inv, my * inv, mz * inv
    third = rho * (1.0 / 3.0)
    pxx = total(e.values()) - third - mx * ux
    pyy = (sy[1] + sy[-1]) - third - my * uy
    pzz = (sz[1] + sz[-1]) - third - mz * uz
    pxy = dy[1] - dy[-1] - mx * uy
    pxz = dz[1] - dz[-1] - mx * uz
    pyz = (s[1, 1] - s[-1, 1]) - (s[1, -1] - s[-1, -1]) - my * uz
    strain = (pxx * pxx + pyy * pyy + pzz * pzz) + 2.0 * (pxy * pxy + pxz * pxz + pyz * pyz)
    size = jnp.sqrt(2.0 * strain)
    tau = 0.5 * (TAU + jnp.sqrt(TAU * TAU + (18.0 * ROOT_TWO * SMAG * SMAG) * size * inv))
    omega = 1.0 / tau
    keep = 1.0 - omega
    base = 1.0 - 1.5 * (ux * ux + uy * uy + uz * uz)
    gain = omega * rho
    gains = [gain * w for w in WEIGHT]
    wx, wy, wz = 3.0 * ux, 3.0 * uy, 3.0 * uz
    t2 = 1.5 * target * target
    t3 = 3.0 * target
    pin_along = {0: 1.0 - t2, 1: 1.0 + t3 + 2.0 * t2, -1: 1.0 - t3 + 2.0 * t2}
    rhos = [rho * w for w in WEIGHT]
    pins = {}
    for cx in SIDES:
        for rest in range(3):
            pins[cx, rest] = rhos[cx * cx + rest] * pin_along[cx]
    post = [None] * 27
    for q in range(13, 27):
        cx, cy, cz = VELOCITY[q]
        kind = cx * cx + cy * cy + cz * cz
        if q == 13:
            post[q] = f[q] * keep + gains[0] * base
        else:
            along = None
            for c, w in ((cx, wx), (cy, wy), (cz, wz)):
                if c:
                    along = (w if c > 0 else -w) if along is None else (along + w if c > 0 else along - w)
            even = base + 0.5 * along * along
            post[q] = f[q] * keep + gains[kind] * (even + along)
            post[26 - q] = f[26 - q] * keep + gains[kind] * (even - along)
    for q in range(27):
        cx, cy, cz = VELOCITY[q]
        post[q] = jnp.where(sponge, pins[cx, cy * cy + cz * cz], post[q])
    return post


def kernel(
    sizes, pops_hbm, solid_hbm, table_hbm, index_hbm, out_ref,
    fin, solid_ref, table_ref, index_ref, target_ref, post, xpk, ypk, zr, yr, er, xr, masks,
    in_sem, send_sem, recv_sem,
):
    nx, ny, nz = sizes
    gx, gy, gz = lax.axis_index("gx"), lax.axis_index("gy"), lax.axis_index("gz")
    at_top, at_bottom = gz == nz - 1, gz == 0

    def neighbour(d):
        dx, dy, dz = d
        px = gx if dx == 0 else lax.rem(gx + (dx + nx), nx)
        py = gy if dy == 0 else lax.rem(gy + (dy + ny), ny)
        return px, py, gz + dz

    def along_z(dz, body):
        if dz == 0:
            body()
        else:
            pl.when(jnp.logical_not(at_top if dz > 0 else at_bottom))(body)

    barrier = pltpu.get_barrier_semaphore()
    for dz in (0, -1, 1):
        def greet(dz=dz):
            for d in FAR_FIRST:
                if d[2] == dz:
                    pl.semaphore_signal(
                        barrier, inc=1, device_id=neighbour(d), device_id_type=pl.DeviceIdType.MESH
                    )
        along_z(dz, greet)

    small = [
        pltpu.make_async_copy(src, dst, in_sem.at[Z + i])
        for i, (src, dst) in enumerate(
            ((index_hbm, index_ref), (table_hbm, table_ref), (solid_hbm, solid_ref))
        )
    ]
    for copy in small:
        copy.start()
    loads = {}
    for z in (0, 3, 1, 2):
        loads[z] = pltpu.make_async_copy(pops_hbm.at[:, z], fin.at[z], in_sem.at[z])
        loads[z].start()

    row = lax.broadcasted_iota(jnp.int32, (Y, X), 0)
    lane = lax.broadcasted_iota(jnp.int32, (Y, X), 1)
    edge_row = {1: row == 0, -1: row == Y - 1}
    edge_lane = {1: lane == 0, -1: lane == X - 1}
    sponge = (lane < SPONGE - gx * X)
    top_mask = (row * 0 + gz) == nz - 1
    bottom_mask = (row * 0 + gz) == 0

    def rows_to(dy):
        return pl.ds(0, Y) if dy == 0 else pl.ds(Y - 1 if dy > 0 else 0, 1)

    def dst_of(step, d):
        dx, dy, dz = d
        if dx:
            return xr.at[step, DIRS.index(d), rows_to(dy)]
        if dy == 0:
            return zr.at[step, (dz + 1) // 2, pl.ds(0, (10 - step) * Y)]
        if dz == 0:
            return yr.at[step, (dy + 1) // 2, pl.ds(0, 40 - 2 * step)]
        return er.at[step, dy + 1 + (dz + 1) // 2, pl.ds(0 if dz > 0 else 4, 4 - step)]

    def src_of(step, d):
        dx, dy, dz = d
        if dx:
            return xpk.at[step, (dx + 1) // 2, rows_to(dy)]
        if dy == 0:
            if dz > 0:
                return post.at[step, Z - 1, pl.ds(19 * Y, (10 - step) * Y)]
            return post.at[step, 0, pl.ds(step * Y, (10 - step) * Y)]
        if dz == 0:
            return ypk.at[step, (dy + 1) // 2, pl.ds(0, 40 - 2 * step)]
        return ypk.at[step, (dy + 1) // 2, pl.ds(0 if dz > 0 else 4, 4 - step)]

    def message(step, d):
        i = DIRS.index(d)
        return pltpu.make_async_remote_copy(
            src_ref=src_of(step, d), dst_ref=dst_of(step, d),
            send_sem=send_sem.at[step, i], recv_sem=recv_sem.at[step, i],
            device_id=neighbour(d), device_id_type=pl.DeviceIdType.MESH,
        )

    def each(step, chosen, what):
        for dz in (0, -1, 1):
            dirs = [d for d in FAR_FIRST if d in chosen and d[2] == dz]
            if dirs:
                def body(dirs=dirs):
                    for d in dirs:
                        getattr(message(step, d), what)()
                along_z(-dz if what == "wait_recv" else dz, body)

    z_dirs = [d for d in DIRS if d[0] == 0 and d[1] == 0]
    y_dirs = [d for d in DIRS if d[0] == 0 and d[1] != 0]
    x_dirs = [d for d in DIRS if d[0] != 0]

    def put(step, z, values):
        for q in range(27):
            post[step, z, (q + 1) * Y:(q + 2) * Y, :] = values[q]

    def tile(step, z, q):
        return post[step, z, (q + 1) * Y:(q + 2) * Y, :]

    def pack(step, packed, z, values, solid):
        for side in (-1, 1):
            acc = packed[side]
            for cy in SIDES:
                for cz in SIDES:
                    col = lane_of(cy, cz, z)
                    shift = (col - (X - 1 if side > 0 else 0)) % X
                    acc = jnp.where(lane == col, pltpu.roll(values[num(side, cy, cz)], shift, 1), acc)
            if step == 0:
                col = 36 + z
                shift = (col - (X - 1 if side > 0 else 0)) % X
                acc = jnp.where(lane == col, pltpu.roll(solid, shift, 1), acc)
            packed[side] = acc
        for side in (-1, 1):
            own = Y - 1 if side > 0 else 0
            for cz in SIDES:
                start = Y_ROW[cz, z]
                first = (num(-1, side, cz) + 1) * Y + own
                ypk[step, (side + 1) // 2, start:start + 3, :] = post[
                    step, z, pl.ds(first, 3, stride=Y), :
                ]
            if step == 0:
                at = Y_SOLID[z]
                ypk[step, (side + 1) // 2, at:at + 1, :] = post[step, z, own:own + 1, :]

    def exchange(step, plane):
        packed = {side: jnp.zeros((Y, X), F32) for side in (-1, 1)}
        for z in (0, 3, 1, 2):
            values = collide(plane(z), target_ref[z], sponge)
            put(step, z, values)
            solid = None
            if step == 0:
                solid = solid_ref[z].astype(F32)
                post[step, z, 0:Y, :] = solid
                post[step, z, 28 * Y:29 * Y, :] = solid
            pack(step, packed, z, values, solid)
            if z == 3 and step == 1:
                each(step, z_dirs, "start")
        for side in (-1, 1):
            xpk[step, (side + 1) // 2] = packed[side]
        if step == 0:
            pl.semaphore_wait(barrier, jnp.where(at_top | at_bottom, 17, 26))
        each(step, x_dirs, "start")
        if step == 0:
            each(step, z_dirs, "start")
        each(step, y_dirs, "start")
        each(step, x_dirs, "wait_recv")
        each(step, y_dirs, "wait_recv")
        each(step, z_dirs, "wait_recv")

    def columns(step):
        result = {}
        for cx in (-1, 1):
            for dz in (0, -1, 1):
                near = xr[step, DIRS.index((cx, 0, dz))]
                for cy in SIDES:
                    got = near
                    if cy:
                        far = xr[step, DIRS.index((cx, cy, dz))]
                        got = pltpu.roll(jnp.where(edge_row[-cy], far, near), cy % Y, 0)
                    if dz == -1:
                        mirrored = pltpu.roll(result[cx, cy, 0], X - 33, 1)
                        got = jnp.where(top_mask, mirrored, got)
                    result[cx, cy, dz] = got
        return result

    def shift(value, cx, cy, line, column, col):
        if cy:
            value = jnp.where(edge_row[cy], line(), pltpu.roll(value, cy % Y, 0))
        if cx:
            spot = 0 if cx > 0 else X - 1
            value = jnp.where(
                edge_lane[cx], pltpu.roll(column, (spot - col) % X, 1), pltpu.roll(value, cx % X, 1)
            )
        return value

    def y_line(step, cy, at):
        return jnp.broadcast_to(yr[step, (cy + 1) // 2, at:at + 1, :], (Y, X))

    def e_line(step, cy, dz, at):
        return jnp.broadcast_to(er[step, cy + 1 + (dz + 1) // 2, at:at + 1, :], (Y, X))

    def build_masks(cols):
        for cx in SIDES:
            for cy in SIDES:
                for z in range(-1, Z + 1):
                    if 0 <= z < Z:
                        dz, col, value = 0, 36 + z, post[0, z, 0:Y, :]
                        line = lambda: y_line(0, cy, Y_SOLID[z])
                    elif z < 0:
                        dz, col, value = 1, 36 + Z - 1, zr[0, 1, 9 * Y:10 * Y, :]
                        line = lambda: e_line(0, cy, 1, 3)
                    else:
                        dz, col, value = -1, 36, zr[0, 0, 0:Y, :]
                        line = lambda: e_line(0, cy, -1, 7)
                    value = shift(value, cx, cy, line, cols.get((cx, cy, dz)), col)
                    if z < 0:
                        value = jnp.where(bottom_mask, 1.0, value)
                    if z == Z:
                        value = jnp.where(top_mask, 0.0, value)
                    masks[(3 * (cy + 1) + cx + 1) * (Z + 2) + z + 1] = value

    def stream(step, z, cols):
        own = post[0, z, 0:Y, :] > 0.5
        result = []
        for q in range(27):
            cx, cy, cz = VELOCITY[q]
            at = z - cz
            if 0 <= at < Z:
                value = tile(step, at, q)
                dz, col = 0, lane_of(cy, cz, at)
                line = lambda: y_line(step, cy, Y_ROW[cz, at] + cx + 1)
            elif at < 0:
                value = zr[step, 1, (q - 18) * Y:(q - 17) * Y, :]
                dz, col = 1, lane_of(cy, cz, Z - 1)
                line = lambda: e_line(step, cy, 1, cx + 1)
            else:
                first = (q + 1 - step) * Y
                value = jnp.where(top_mask, tile(step, Z - 1, num(cx, cy, 1)), zr[step, 0, first:first + Y, :])
                dz, col = -1, lane_of(cy, cz, 0)
                line = lambda: jnp.where(
                    top_mask, y_line(step, cy, Y_ROW[1, Z - 1] + cx + 1), e_line(step, cy, -1, 4 + cx + 1)
                )
            value = shift(value, cx, cy, line, cols.get((cx, cy, dz)), col)
            if q != 13:
                blocked = masks[(3 * (cy + 1) + cx + 1) * (Z + 2) + at + 1] > 0.5
                value = jnp.where(blocked, tile(step, z, 26 - q), value)
            result.append(jnp.where(own, weight(q), value))
        return result

    def first_plane(z):
        loads[z].wait()
        return [fin[z, q] for q in range(27)]

    for copy in small:
        copy.wait()
    which = row * 0
    for y in range(Y):
        which = jnp.where(row == y, index_ref[y], which)
    for z in range(Z):
        target = jnp.zeros((Y, X), F32)
        for p in range(table_ref.shape[1]):
            entry = jnp.broadcast_to(table_ref[z:z + 1, p:p + 1], (Y, X))
            target = jnp.where(which == p, entry, target)
        target_ref[z] = target
    exchange(0, first_plane)
    cols = columns(0)
    build_masks(cols)
    exchange(1, lambda z: stream(0, z, cols))
    cols = columns(1)
    for z in range(Z):
        values = stream(1, z, cols)
        for q in range(27):
            out_ref[q, z] = values[q]
    for step in range(2):
        for dirs in (z_dirs, y_dirs, x_dirs):
            each(step, dirs, "wait_send")


def shards(mesh_shape, pops, solid, profile_table, profile_index):
    vmem = pl.BlockSpec(memory_space=pltpu.VMEM)
    return pl.pallas_call(
        functools.partial(kernel, mesh_shape),
        out_shape=jax.ShapeDtypeStruct(pops.shape, F32),
        in_specs=[pl.BlockSpec(memory_space=pltpu.HBM)] * 4,
        out_specs=vmem,
        scratch_shapes=[
            pltpu.VMEM((Z, 27, Y, X), F32),
            pltpu.VMEM((Z, Y, X), jnp.int32),
            pltpu.VMEM((Z, profile_table.shape[0]), F32),
            pltpu.SMEM((Y,), jnp.int32),
            pltpu.VMEM((Z, Y, X), F32),
            pltpu.VMEM((2, Z, 29 * Y, X), F32),
            pltpu.VMEM((2, 2, Y, X), F32),
            pltpu.VMEM((2, 2, 40, X), F32),
            pltpu.VMEM((2, 2, 10 * Y, X), F32),
            pltpu.VMEM((2, 2, 40, X), F32),
            pltpu.VMEM((2, 4, Y, X), F32),
            pltpu.VMEM((2, 26, Y, X), F32),
            pltpu.VMEM((9 * (Z + 2), Y, X), F32),
            pltpu.SemaphoreType.DMA((Z + 3,)),
            pltpu.SemaphoreType.DMA((2, 26)),
            pltpu.SemaphoreType.DMA((2, 26)),
        ],
        compiler_params=pltpu.CompilerParams(
            collective_id=0, has_side_effects=True, vmem_limit_bytes=32 * 1024 * 1024
        ),
    )(*[pltpu.with_memory_space_constraint(a, pltpu.HBM) for a in (pops, solid, profile_table.T, profile_index)])


def solution(mesh):
    sizes = tuple(mesh.shape[axis] for axis in ("gx", "gy", "gz"))
    return jax.shard_map(
        functools.partial(shards, sizes),
        mesh=mesh,
        in_specs=(P(None, "gz", "gy", "gx"), P("gz", "gy", "gx"), P(None, "gz"), P("gy")),
        out_specs=P(None, "gz", "gy", "gx"),
        check_vma=False,
    )
```

```python
import functools

import jax
import jax.numpy as jnp
from jax import lax
from jax.experimental import pallas as pl
from jax.experimental.pallas import tpu as pltpu
from jax.sharding import PartitionSpec as P

SPONGE = 32
TAU = 0.52
SMAG = 0.17
ROOT_TWO = 1.4142135623730951
WEIGHT = (8.0 / 27.0, 2.0 / 27.0, 1.0 / 54.0, 1.0 / 216.0)
F32 = jnp.float32
SIDES = (-1, 0, 1)
VELOCITY = [(cx, cy, cz) for cz in SIDES for cy in SIDES for cx in SIDES]
DIRS = [(dx, dy, dz) for dx in SIDES for dy in SIDES for dz in SIDES if (dx, dy, dz) != (0, 0, 0)]
FAR_FIRST = sorted(DIRS, key=lambda d: (d[0] == 0, d[1] == 0, d[2] == 0))
Z = 4
Y = 8
X = 128


def num(cx, cy, cz):
    return 9 * (cz + 1) + 3 * (cy + 1) + cx + 1


def weight(q):
    return WEIGHT[sum(c * c for c in VELOCITY[q])]


def lane_of(cy, cz, z):
    return 9 * z + 3 * (cz + 1) + cy + 1


def y_groups():
    table, row = {(1, Z - 1): 0, (-1, 0): 4}, 8
    for z in range(Z):
        for cz in SIDES:
            if (cz, z) not in table:
                table[cz, z] = row
                row += 3
    solid = {Z - 1: 3, 0: 7}
    for z in range(1, Z - 1):
        solid[z] = row
        row += 1
    assert row == 40
    return table, solid


Y_ROW, Y_SOLID = y_groups()


def total(values):
    values = list(values)
    while len(values) > 1:
        values = [a + b for a, b in zip(values[::2], values[1::2])] + (
            [values[-1]] if len(values) % 2 else []
        )
    return values[0]


def collide(f, target, sponge):
    s, d, e = {}, {}, {}
    for cz in SIDES:
        for cy in SIDES:
            lo, mid, hi = (f[num(cx, cy, cz)] for cx in SIDES)
            e[cy, cz] = hi + lo
            s[cy, cz] = e[cy, cz] + mid
            d[cy, cz] = hi - lo
    sy = {cy: total(s[cy, cz] for cz in SIDES) for cy in SIDES}
    sz = {cz: total(s[cy, cz] for cy in SIDES) for cz in SIDES}
    dy = {cy: total(d[cy, cz] for cz in SIDES) for cy in SIDES}
    dz = {cz: total(d[cy, cz] for cy in SIDES) for cz in (-1, 1)}
    rho = sy[-1] + sy[0] + sy[1]
    mx, my, mz = dy[-1] + dy[0] + dy[1], sy[1] - sy[-1], sz[1] - sz[-1]
    inv = 1.0 / rho
    ux, uy, uz = mx * inv, my * inv, mz * inv
    third = rho * (1.0 / 3.0)
    pxx = total(e.values()) - third - mx * ux
    pyy = (sy[1] + sy[-1]) - third - my * uy
    pzz = (sz[1] + sz[-1]) - third - mz * uz
    pxy = dy[1] - dy[-1] - mx * uy
    pxz = dz[1] - dz[-1] - mx * uz
    pyz = (s[1, 1] - s[-1, 1]) - (s[1, -1] - s[-1, -1]) - my * uz
    strain = (pxx * pxx + pyy * pyy + pzz * pzz) + 2.0 * (pxy * pxy + pxz * pxz + pyz * pyz)
    size = jnp.sqrt(2.0 * strain)
    tau = 0.5 * (TAU + jnp.sqrt(TAU * TAU + (18.0 * ROOT_TWO * SMAG * SMAG) * size * inv))
    omega = 1.0 / tau
    keep = 1.0 - omega
    base = 1.0 - 1.5 * (ux * ux + uy * uy + uz * uz)
    gain = omega * rho
    gains = [gain * w for w in WEIGHT]
    wx, wy, wz = 3.0 * ux, 3.0 * uy, 3.0 * uz
    t2 = 1.5 * target * target
    t3 = 3.0 * target
    pin_along = {0: 1.0 - t2, 1: 1.0 + t3 + 2.0 * t2, -1: 1.0 - t3 + 2.0 * t2}
    rhos = [rho * w for w in WEIGHT]
    pins = {}
    for cx in SIDES:
        for rest in range(3):
            pins[cx, rest] = rhos[cx * cx + rest] * pin_along[cx]
    post = [None] * 27
    for q in range(13, 27):
        cx, cy, cz = VELOCITY[q]
        kind = cx * cx + cy * cy + cz * cz
        if q == 13:
            post[q] = f[q] * keep + gains[0] * base
        else:
            along = None
            for c, w in ((cx, wx), (cy, wy), (cz, wz)):
                if c:
                    along = (w if c > 0 else -w) if along is None else (along + w if c > 0 else along - w)
            even = base + 0.5 * along * along
            post[q] = f[q] * keep + gains[kind] * (even + along)
            post[26 - q] = f[26 - q] * keep + gains[kind] * (even - along)
    for q in range(27):
        cx, cy, cz = VELOCITY[q]
        post[q] = jnp.where(sponge, pins[cx, cy * cy + cz * cz], post[q])
    return post


def streaming(step, pre, post, zr, yr, er, xr, masks, own_ref, at_top, at_bottom):
    row = lax.broadcasted_iota(jnp.int32, (Y, X), 0)
    lane = lax.broadcasted_iota(jnp.int32, (Y, X), 1)
    edge_row = {1: row == 0, -1: row == Y - 1}
    edge_lane = {1: lane == 0, -1: lane == X - 1}
    top_mask = (row * 0 + at_top.astype(jnp.int32)) == 1
    bottom_mask = (row * 0 + at_bottom.astype(jnp.int32)) == 1

    def tile(z, q):
        return post[z, (q + 1) * Y:(q + 2) * Y, :]

    def columns():
        result = {}
        for cx in (-1, 1):
            for dz in (0, -1, 1):
                near = xr[DIRS.index((cx, 0, dz))]
                for cy in SIDES:
                    got = near
                    if cy:
                        far = xr[DIRS.index((cx, cy, dz))]
                        got = pltpu.roll(jnp.where(edge_row[-cy], far, near), cy % Y, 0)
                    if dz == -1:
                        mirrored = pltpu.roll(result[cx, cy, 0], X - 33, 1)
                        got = jnp.where(top_mask, mirrored, got)
                    result[cx, cy, dz] = got
        return result

    def moved(value, cx, cy, line):
        if cy:
            value = jnp.where(edge_row[cy], line(), pltpu.roll(value, cy % Y, 0))
        return pltpu.roll(value, cx % X, 1) if cx else value

    def joined(value, cx, column, col):
        spot = 0 if cx > 0 else X - 1
        return jnp.where(edge_lane[cx], pltpu.roll(column, (spot - col) % X, 1), value)

    def y_line(cy, at):
        return jnp.broadcast_to(yr[(cy + 1) // 2, at:at + 1, :], (Y, X))

    def e_line(cy, dz, at):
        return jnp.broadcast_to(er[cy + 1 + (dz + 1) // 2, at:at + 1, :], (Y, X))

    def closed(value, z):
        if z < 0:
            return jnp.where(bottom_mask, 1.0, value)
        return jnp.where(top_mask, 0.0, value) if z == Z else value

    def mask_at(cx, cy, z):
        return (3 * (cy + 1) + cx + 1) * (Z + 2) + z + 1

    def early_masks():
        for cy in SIDES:
            for z in range(-1, Z + 1):
                if 0 <= z < Z:
                    value = own_ref[z]
                    line = lambda: y_line(cy, Y_SOLID[z])
                elif z < 0:
                    value = zr[1, 9 * Y:10 * Y, :]
                    line = lambda: e_line(cy, 1, 3)
                else:
                    value = zr[0, 0:Y, :]
                    line = lambda: e_line(cy, -1, 7)
                value = moved(value, 0, cy, line)
                for cx in SIDES:
                    got = moved(value, cx, 0, None)
                    masks[mask_at(cx, cy, z)] = got if cx else closed(got, z)

    def late_masks(cols):
        for cx in (-1, 1):
            for cy in SIDES:
                for z in range(-1, Z + 1):
                    dz, col = (0, 36 + z) if 0 <= z < Z else (1, 36 + Z - 1) if z < 0 else (-1, 36)
                    at = mask_at(cx, cy, z)
                    masks[at] = closed(joined(masks[at], cx, cols[cx, cy, dz], col), z)

    def settled(value, z, q):
        cx, cy, cz = VELOCITY[q]
        if q != 13:
            blocked = masks[mask_at(cx, cy, z - cz)] > 0.5
            value = jnp.where(blocked, tile(z, 26 - q), value)
        return jnp.where(own_ref[z] > 0.5, weight(q), value)

    def early(z):
        for q in range(27):
            cx, cy, cz = VELOCITY[q]
            at = z - cz
            if 0 <= at < Z:
                value = tile(at, q)
                line = lambda: y_line(cy, Y_ROW[cz, at] + cx + 1)
            elif at < 0:
                value = zr[1, (q - 18) * Y:(q - 17) * Y, :]
                line = lambda: e_line(cy, 1, cx + 1)
            else:
                first = (q + 1 - step) * Y
                value = jnp.where(top_mask, tile(Z - 1, num(cx, cy, 1)), zr[0, first:first + Y, :])
                line = lambda: jnp.where(
                    top_mask, y_line(cy, Y_ROW[1, Z - 1] + cx + 1), e_line(cy, -1, 4 + cx + 1)
                )
            value = moved(value, cx, cy, line)
            pre[z, q] = value if cx else settled(value, z, q)

    def late(z, cols):
        result = []
        for q in range(27):
            cx, cy, cz = VELOCITY[q]
            value = pre[z, q]
            if cx:
                at = z - cz
                dz, source = (0, at) if 0 <= at < Z else (1, Z - 1) if at < 0 else (-1, 0)
                value = joined(value, cx, cols[cx, cy, dz], lane_of(cy, cz, source))
                value = settled(value, z, q)
            result.append(value)
        return result

    return columns, early_masks, late_masks, early, late


def kernel(
    sizes, pops_hbm, solid_hbm, table_hbm, index_hbm,
    pre1, post1, zr1, yr1, er1, xr1, masks, own_ref,
    fin, solid_ref, table_ref, index_ref, target_ref, pre0, post0, zr0, yr0, er0, xr0, xpk, ypk,
    in_sem, send_sem, recv_sem,
):
    nx, ny, nz = sizes
    post, zr, yr, er, xr = (post0, post1), (zr0, zr1), (yr0, yr1), (er0, er1), (xr0, xr1)
    gx, gy, gz = lax.axis_index("gx"), lax.axis_index("gy"), lax.axis_index("gz")
    at_top, at_bottom = gz == nz - 1, gz == 0

    def neighbour(d):
        dx, dy, dz = d
        px = gx if dx == 0 else lax.rem(gx + (dx + nx), nx)
        py = gy if dy == 0 else lax.rem(gy + (dy + ny), ny)
        return px, py, gz + dz

    def along_z(dz, body):
        if dz == 0:
            body()
        else:
            pl.when(jnp.logical_not(at_top if dz > 0 else at_bottom))(body)

    barrier = pltpu.get_barrier_semaphore()
    for dz in (0, -1, 1):
        def greet(dz=dz):
            for d in FAR_FIRST:
                if d[2] == dz:
                    pl.semaphore_signal(
                        barrier, inc=1, device_id=neighbour(d), device_id_type=pl.DeviceIdType.MESH
                    )
        along_z(dz, greet)

    small = [
        pltpu.make_async_copy(src, dst, in_sem.at[Z + i])
        for i, (src, dst) in enumerate(
            ((index_hbm, index_ref), (table_hbm, table_ref), (solid_hbm, solid_ref))
        )
    ]
    for copy in small:
        copy.start()
    loads = {}
    for z in (0, 3, 1, 2):
        loads[z] = pltpu.make_async_copy(pops_hbm.at[:, z], fin.at[z], in_sem.at[z])
        loads[z].start()

    row = lax.broadcasted_iota(jnp.int32, (Y, X), 0)
    lane = lax.broadcasted_iota(jnp.int32, (Y, X), 1)
    sponge = (lane < SPONGE - gx * X)

    def rows_to(dy):
        return pl.ds(0, Y) if dy == 0 else pl.ds(Y - 1 if dy > 0 else 0, 1)

    def dst_of(step, d):
        dx, dy, dz = d
        if dx:
            return xr[step].at[DIRS.index(d), rows_to(dy)]
        if dy == 0:
            return zr[step].at[(dz + 1) // 2, pl.ds(0, (10 - step) * Y)]
        if dz == 0:
            return yr[step].at[(dy + 1) // 2, pl.ds(0, 40 - 2 * step)]
        return er[step].at[dy + 1 + (dz + 1) // 2, pl.ds(0 if dz > 0 else 4, 4 - step)]

    def src_of(step, d):
        dx, dy, dz = d
        if dx:
            return xpk.at[step, (dx + 1) // 2, rows_to(dy)]
        if dy == 0:
            if dz > 0:
                return post[step].at[Z - 1, pl.ds(19 * Y, (10 - step) * Y)]
            return post[step].at[0, pl.ds(step * Y, (10 - step) * Y)]
        if dz == 0:
            return ypk.at[step, (dy + 1) // 2, pl.ds(0, 40 - 2 * step)]
        return ypk.at[step, (dy + 1) // 2, pl.ds(0 if dz > 0 else 4, 4 - step)]

    def message(step, d):
        i = DIRS.index(d)
        return pltpu.make_async_remote_copy(
            src_ref=src_of(step, d), dst_ref=dst_of(step, d),
            send_sem=send_sem.at[step, i], recv_sem=recv_sem.at[step, i],
            device_id=neighbour(d), device_id_type=pl.DeviceIdType.MESH,
        )

    def each(step, chosen, what):
        for dz in (0, -1, 1):
            dirs = [d for d in FAR_FIRST if d in chosen and d[2] == dz]
            if dirs:
                def body(dirs=dirs):
                    for d in dirs:
                        getattr(message(step, d), what)()
                along_z(-dz if what == "wait_recv" else dz, body)

    z_dirs = [d for d in DIRS if d[0] == 0 and d[1] == 0]
    y_dirs = [d for d in DIRS if d[0] == 0 and d[1] != 0]
    x_dirs = [d for d in DIRS if d[0] != 0]

    def put(step, z, values):
        for q in range(27):
            post[step][z, (q + 1) * Y:(q + 2) * Y, :] = values[q]

    def pack(step, packed, z, values, solid):
        for side in (-1, 1):
            acc = packed[side]
            for cy in SIDES:
                for cz in SIDES:
                    col = lane_of(cy, cz, z)
                    shift = (col - (X - 1 if side > 0 else 0)) % X
                    acc = jnp.where(lane == col, pltpu.roll(values[num(side, cy, cz)], shift, 1), acc)
            if step == 0:
                col = 36 + z
                shift = (col - (X - 1 if side > 0 else 0)) % X
                acc = jnp.where(lane == col, pltpu.roll(solid, shift, 1), acc)
            packed[side] = acc
        for side in (-1, 1):
            own = Y - 1 if side > 0 else 0
            for cz in SIDES:
                start = Y_ROW[cz, z]
                first = (num(-1, side, cz) + 1) * Y + own
                ypk[step, (side + 1) // 2, start:start + 3, :] = post[step][
                    z, pl.ds(first, 3, stride=Y), :
                ]
            if step == 0:
                at = Y_SOLID[z]
                ypk[step, (side + 1) // 2, at:at + 1, :] = post[step][z, own:own + 1, :]

    def exchange(step, plane):
        packed = {side: jnp.zeros((Y, X), F32) for side in (-1, 1)}
        for z in (0, 3, 1, 2):
            values = collide(plane(z), target_ref[z], sponge)
            put(step, z, values)
            solid = None
            if step == 0:
                solid = solid_ref[z].astype(F32)
                post[step][z, 0:Y, :] = solid
                own_ref[z] = solid
                post[step][z, 28 * Y:29 * Y, :] = solid
            pack(step, packed, z, values, solid)
            if z == 3 and step == 1:
                each(step, z_dirs, "start")
        for side in (-1, 1):
            xpk[step, (side + 1) // 2] = packed[side]
        if step == 0:
            pl.semaphore_wait(barrier, jnp.where(at_top | at_bottom, 17, 26))
        each(step, x_dirs, "start")
        if step == 0:
            each(step, z_dirs, "start")
        each(step, y_dirs, "start")
        each(step, y_dirs, "wait_recv")
        each(step, z_dirs, "wait_recv")
        if step == 0:
            early_masks[0]()
        for z in range(Z):
            early[step](z)
        each(step, x_dirs, "wait_recv")

    def first_plane(z):
        loads[z].wait()
        return [fin[z, q] for q in range(27)]

    for copy in small:
        copy.wait()
    which = row * 0
    for y in range(Y):
        which = jnp.where(row == y, index_ref[y], which)
    for z in range(Z):
        target = jnp.zeros((Y, X), F32)
        for p in range(table_ref.shape[1]):
            entry = jnp.broadcast_to(table_ref[z:z + 1, p:p + 1], (Y, X))
            target = jnp.where(which == p, entry, target)
        target_ref[z] = target
    columns, early_masks, late_masks, early, late = zip(*(
        streaming(
            step, (pre0, pre1)[step], post[step], zr[step], yr[step], er[step], xr[step],
            masks, own_ref, at_top, at_bottom,
        )
        for step in range(2)
    ))
    exchange(0, first_plane)
    cols = columns[0]()
    late_masks[0](cols)
    exchange(1, lambda z: late[0](z, cols))
    for step in range(2):
        for dirs in (z_dirs, y_dirs, x_dirs):
            each(step, dirs, "wait_send")


def last(nz, pre, post, zr, yr, er, xr, masks, own_ref, out_hbm, buf, sem):
    gz = lax.axis_index("gz")
    columns, _, _, _, late = streaming(
        1, pre, post, zr, yr, er, xr, masks, own_ref, gz == nz - 1, gz == 0
    )
    cols = columns()
    copies = []
    for z in range(Z):
        values = late(z, cols)
        for q in range(27):
            buf[z, q] = values[q]
        copies.append(pltpu.make_async_copy(buf.at[z], out_hbm.at[:, z], sem.at[z]))
        copies[-1].start()
    for copy in copies:
        copy.wait()


def shards(mesh_shape, pops, solid, profile_table, profile_index):
    vmem = pl.BlockSpec(memory_space=pltpu.VMEM)
    step_shapes = [(Z, 27, Y, X), (Z, 29 * Y, X), (2, 10 * Y, X), (2, 40, X), (4, Y, X), (26, Y, X)]
    kept_shapes = step_shapes + [(9 * (Z + 2), Y, X), (Z, Y, X)]
    kept = pl.pallas_call(
        functools.partial(kernel, mesh_shape),
        out_shape=[jax.ShapeDtypeStruct(shape, F32) for shape in kept_shapes],
        in_specs=[pl.BlockSpec(memory_space=pltpu.HBM)] * 4,
        out_specs=[vmem] * len(kept_shapes),
        scratch_shapes=[
            pltpu.VMEM((Z, 27, Y, X), F32),
            pltpu.VMEM((Z, Y, X), jnp.int32),
            pltpu.VMEM((Z, profile_table.shape[0]), F32),
            pltpu.SMEM((Y,), jnp.int32),
            pltpu.VMEM((Z, Y, X), F32),
            *[pltpu.VMEM(shape, F32) for shape in step_shapes],
            pltpu.VMEM((2, 2, Y, X), F32),
            pltpu.VMEM((2, 2, 40, X), F32),
            pltpu.SemaphoreType.DMA((Z + 3,)),
            pltpu.SemaphoreType.DMA((2, 26)),
            pltpu.SemaphoreType.DMA((2, 26)),
        ],
        compiler_params=pltpu.CompilerParams(
            collective_id=0, has_side_effects=True, vmem_limit_bytes=32 * 1024 * 1024
        ),
    )(*[
        pltpu.with_memory_space_constraint(a, pltpu.HBM)
        for a in (pops, solid, profile_table.T, profile_index)
    ])
    return pl.pallas_call(
        functools.partial(last, mesh_shape[2]),
        out_shape=jax.ShapeDtypeStruct(pops.shape, F32),
        in_specs=[vmem] * len(kept_shapes),
        out_specs=pl.BlockSpec(memory_space=pl.ANY),
        scratch_shapes=[pltpu.VMEM((Z, 27, Y, X), F32), pltpu.SemaphoreType.DMA((Z,))],
        compiler_params=pltpu.CompilerParams(vmem_limit_bytes=32 * 1024 * 1024),
    )(*kept)


def solution(mesh):
    sizes = tuple(mesh.shape[axis] for axis in ("gx", "gy", "gz"))
    return jax.shard_map(
        functools.partial(shards, sizes),
        mesh=mesh,
        in_specs=(P(None, "gz", "gy", "gx"), P("gz", "gy", "gx"), P(None, "gz"), P("gy")),
        out_specs=P(None, "gz", "gy", "gx"),
        check_vma=False,
    )
```

```python
import functools

import jax
import jax.numpy as jnp
from jax import lax
from jax.experimental import pallas as pl
from jax.experimental.pallas import tpu as pltpu
from jax.sharding import PartitionSpec as P

SPONGE = 32
TAU = 0.52
SMAG = 0.17
ROOT_TWO = 1.4142135623730951
WEIGHT = (8.0 / 27.0, 2.0 / 27.0, 1.0 / 54.0, 1.0 / 216.0)
F32 = jnp.float32
SIDES = (-1, 0, 1)
VELOCITY = [(cx, cy, cz) for cz in SIDES for cy in SIDES for cx in SIDES]
DIRS = [(dx, dy, dz) for dx in SIDES for dy in SIDES for dz in SIDES if (dx, dy, dz) != (0, 0, 0)]
FAR_FIRST = sorted(DIRS, key=lambda d: (d[0] == 0, d[1] == 0, d[2] == 0))
Z = 4
Y = 8
X = 128


def num(cx, cy, cz):
    return 9 * (cz + 1) + 3 * (cy + 1) + cx + 1


def weight(q):
    return WEIGHT[sum(c * c for c in VELOCITY[q])]


def lane_of(cy, cz, z):
    return 9 * z + 3 * (cz + 1) + cy + 1


def y_groups():
    table, row = {(1, Z - 1): 0, (-1, 0): 4}, 8
    for z in range(Z):
        for cz in SIDES:
            if (cz, z) not in table:
                table[cz, z] = row
                row += 3
    solid = {Z - 1: 3, 0: 7}
    for z in range(1, Z - 1):
        solid[z] = row
        row += 1
    assert row == 40
    return table, solid


Y_ROW, Y_SOLID = y_groups()


def total(values):
    values = list(values)
    while len(values) > 1:
        values = [a + b for a, b in zip(values[::2], values[1::2])] + (
            [values[-1]] if len(values) % 2 else []
        )
    return values[0]


def collide(f, target, sponge):
    s, d, e = {}, {}, {}
    for cz in SIDES:
        for cy in SIDES:
            lo, mid, hi = (f[num(cx, cy, cz)] for cx in SIDES)
            e[cy, cz] = hi + lo
            s[cy, cz] = e[cy, cz] + mid
            d[cy, cz] = hi - lo
    sy = {cy: total(s[cy, cz] for cz in SIDES) for cy in SIDES}
    sz = {cz: total(s[cy, cz] for cy in SIDES) for cz in SIDES}
    dy = {cy: total(d[cy, cz] for cz in SIDES) for cy in SIDES}
    dz = {cz: total(d[cy, cz] for cy in SIDES) for cz in (-1, 1)}
    rho = sy[-1] + sy[0] + sy[1]
    mx, my, mz = dy[-1] + dy[0] + dy[1], sy[1] - sy[-1], sz[1] - sz[-1]
    inv = 1.0 / rho
    ux, uy, uz = mx * inv, my * inv, mz * inv
    third = rho * (1.0 / 3.0)
    pxx = total(e.values()) - third - mx * ux
    pyy = (sy[1] + sy[-1]) - third - my * uy
    pzz = (sz[1] + sz[-1]) - third - mz * uz
    pxy = dy[1] - dy[-1] - mx * uy
    pxz = dz[1] - dz[-1] - mx * uz
    pyz = (s[1, 1] - s[-1, 1]) - (s[1, -1] - s[-1, -1]) - my * uz
    strain = (pxx * pxx + pyy * pyy + pzz * pzz) + 2.0 * (pxy * pxy + pxz * pxz + pyz * pyz)
    size = jnp.sqrt(2.0 * strain)
    tau = 0.5 * (TAU + jnp.sqrt(TAU * TAU + (18.0 * ROOT_TWO * SMAG * SMAG) * size * inv))
    omega = 1.0 / tau
    keep = 1.0 - omega
    base = 1.0 - 1.5 * (ux * ux + uy * uy + uz * uz)
    gain = omega * rho
    gains = [gain * w for w in WEIGHT]
    wx, wy, wz = 3.0 * ux, 3.0 * uy, 3.0 * uz
    t2 = 1.5 * target * target
    t3 = 3.0 * target
    pin_along = {0: 1.0 - t2, 1: 1.0 + t3 + 2.0 * t2, -1: 1.0 - t3 + 2.0 * t2}
    rhos = [rho * w for w in WEIGHT]
    pins = {}
    for cx in SIDES:
        for rest in range(3):
            pins[cx, rest] = rhos[cx * cx + rest] * pin_along[cx]
    post = [None] * 27
    for q in range(13, 27):
        cx, cy, cz = VELOCITY[q]
        kind = cx * cx + cy * cy + cz * cz
        if q == 13:
            post[q] = f[q] * keep + gains[0] * base
        else:
            along = None
            for c, w in ((cx, wx), (cy, wy), (cz, wz)):
                if c:
                    along = (w if c > 0 else -w) if along is None else (along + w if c > 0 else along - w)
            even = base + 0.5 * along * along
            post[q] = f[q] * keep + gains[kind] * (even + along)
            post[26 - q] = f[26 - q] * keep + gains[kind] * (even - along)
    for q in range(27):
        cx, cy, cz = VELOCITY[q]
        post[q] = jnp.where(sponge, pins[cx, cy * cy + cz * cz], post[q])
    return post


def streaming(step, pre, post, zr, yr, er, xr, masks, own_ref, at_top, at_bottom):
    row = lax.broadcasted_iota(jnp.int32, (Y, X), 0)
    lane = lax.broadcasted_iota(jnp.int32, (Y, X), 1)
    edge_row = {1: row == 0, -1: row == Y - 1}
    edge_lane = {1: lane == 0, -1: lane == X - 1}
    top_mask = (row * 0 + at_top.astype(jnp.int32)) == 1
    bottom_mask = (row * 0 + at_bottom.astype(jnp.int32)) == 1

    def tile(z, q):
        return post[z, (q + 1) * Y:(q + 2) * Y, :]

    def columns():
        result = {}
        for cx in (-1, 1):
            for dz in (0, -1, 1):
                near = xr[DIRS.index((cx, 0, dz))]
                for cy in SIDES:
                    got = near
                    if cy:
                        far = xr[DIRS.index((cx, cy, dz))]
                        got = pltpu.roll(jnp.where(edge_row[-cy], far, near), cy % Y, 0)
                    if dz == -1:
                        mirrored = pltpu.roll(result[cx, cy, 0], X - 33, 1)
                        got = jnp.where(top_mask, mirrored, got)
                    result[cx, cy, dz] = got
        return result

    def moved(value, cx, cy, line):
        if cy:
            value = jnp.where(edge_row[cy], line(), pltpu.roll(value, cy % Y, 0))
        return pltpu.roll(value, cx % X, 1) if cx else value

    def joined(value, cx, column, col):
        spot = 0 if cx > 0 else X - 1
        return jnp.where(edge_lane[cx], pltpu.roll(column, (spot - col) % X, 1), value)

    def y_line(cy, at):
        return jnp.broadcast_to(yr[(cy + 1) // 2, at:at + 1, :], (Y, X))

    def e_line(cy, dz, at):
        return jnp.broadcast_to(er[cy + 1 + (dz + 1) // 2, at:at + 1, :], (Y, X))

    def closed(value, z):
        if z < 0:
            return jnp.where(bottom_mask, 1.0, value)
        return jnp.where(top_mask, 0.0, value) if z == Z else value

    def mask_at(cx, cy, z):
        return (3 * (cy + 1) + cx + 1) * (Z + 2) + z + 1

    def early_masks():
        for cy in SIDES:
            for z in range(-1, Z + 1):
                if 0 <= z < Z:
                    value = own_ref[z]
                    line = lambda: y_line(cy, Y_SOLID[z])
                elif z < 0:
                    value = zr[1, 9 * Y:10 * Y, :]
                    line = lambda: e_line(cy, 1, 3)
                else:
                    value = zr[0, 0:Y, :]
                    line = lambda: e_line(cy, -1, 7)
                value = moved(value, 0, cy, line)
                for cx in SIDES:
                    got = moved(value, cx, 0, None)
                    masks[mask_at(cx, cy, z)] = got if cx else closed(got, z)

    def late_masks(cols):
        for cx in (-1, 1):
            for cy in SIDES:
                for z in range(-1, Z + 1):
                    dz, col = (0, 36 + z) if 0 <= z < Z else (1, 36 + Z - 1) if z < 0 else (-1, 36)
                    at = mask_at(cx, cy, z)
                    masks[at] = closed(joined(masks[at], cx, cols[cx, cy, dz], col), z)

    def settled(value, z, q):
        cx, cy, cz = VELOCITY[q]
        if q != 13:
            blocked = masks[mask_at(cx, cy, z - cz)] > 0.5
            value = jnp.where(blocked, tile(z, 26 - q), value)
        return jnp.where(own_ref[z] > 0.5, weight(q), value)

    def early(z):
        for q in range(27):
            cx, cy, cz = VELOCITY[q]
            at = z - cz
            if 0 <= at < Z:
                value = tile(at, q)
                line = lambda: y_line(cy, Y_ROW[cz, at] + cx + 1)
            elif at < 0:
                value = zr[1, (q - 18) * Y:(q - 17) * Y, :]
                line = lambda: e_line(cy, 1, cx + 1)
            else:
                first = (q + 1 - step) * Y
                value = jnp.where(top_mask, tile(Z - 1, num(cx, cy, 1)), zr[0, first:first + Y, :])
                line = lambda: jnp.where(
                    top_mask, y_line(cy, Y_ROW[1, Z - 1] + cx + 1), e_line(cy, -1, 4 + cx + 1)
                )
            value = moved(value, cx, cy, line)
            pre[z, q] = value if cx else settled(value, z, q)

    def late(z, cols):
        result = []
        for q in range(27):
            cx, cy, cz = VELOCITY[q]
            value = pre[z, q]
            if cx:
                at = z - cz
                dz, source = (0, at) if 0 <= at < Z else (1, Z - 1) if at < 0 else (-1, 0)
                value = joined(value, cx, cols[cx, cy, dz], lane_of(cy, cz, source))
                value = settled(value, z, q)
            result.append(value)
        return result

    return columns, early_masks, late_masks, early, late


def kernel(
    sizes, pops_hbm, solid_hbm, table_hbm, index_hbm,
    pre1, post1, zr1, yr1, er1, xr1, masks, own_ref,
    fin, solid_ref, table_ref, index_ref, target_ref, pre0, post0, zr0, yr0, er0, xr0, xpk, ypk,
    in_sem, send_sem, recv_sem,
):
    nx, ny, nz = sizes
    post, zr, yr, er, xr = (post0, post1), (zr0, zr1), (yr0, yr1), (er0, er1), (xr0, xr1)
    gx, gy, gz = lax.axis_index("gx"), lax.axis_index("gy"), lax.axis_index("gz")
    at_top, at_bottom = gz == nz - 1, gz == 0

    def neighbour(d):
        dx, dy, dz = d
        px = gx if dx == 0 else lax.rem(gx + (dx + nx), nx)
        py = gy if dy == 0 else lax.rem(gy + (dy + ny), ny)
        return px, py, gz + dz

    def along_z(dz, body):
        if dz == 0:
            body()
        else:
            pl.when(jnp.logical_not(at_top if dz > 0 else at_bottom))(body)

    barrier = pltpu.get_barrier_semaphore()
    for dz in (0, -1, 1):
        def greet(dz=dz):
            for d in FAR_FIRST:
                if d[2] == dz:
                    pl.semaphore_signal(
                        barrier, inc=1, device_id=neighbour(d), device_id_type=pl.DeviceIdType.MESH
                    )
        along_z(dz, greet)

    small = [
        pltpu.make_async_copy(src, dst, in_sem.at[Z + i])
        for i, (src, dst) in enumerate(
            ((index_hbm, index_ref), (table_hbm, table_ref), (solid_hbm, solid_ref))
        )
    ]
    for copy in small:
        copy.start()
    loads = {}
    for z in (0, 3, 1, 2):
        loads[z] = pltpu.make_async_copy(pops_hbm.at[:, z], fin.at[z], in_sem.at[z])
        loads[z].start()

    row = lax.broadcasted_iota(jnp.int32, (Y, X), 0)
    lane = lax.broadcasted_iota(jnp.int32, (Y, X), 1)
    sponge = (lane < SPONGE - gx * X)

    def rows_to(dy):
        return pl.ds(0, Y) if dy == 0 else pl.ds(Y - 1 if dy > 0 else 0, 1)

    def dst_of(step, d):
        dx, dy, dz = d
        if dx:
            return xr[step].at[DIRS.index(d), rows_to(dy)]
        if dy == 0:
            return zr[step].at[(dz + 1) // 2, pl.ds(0, (10 - step) * Y)]
        if dz == 0:
            return yr[step].at[(dy + 1) // 2, pl.ds(0, 40 - 2 * step)]
        return er[step].at[dy + 1 + (dz + 1) // 2, pl.ds(0 if dz > 0 else 4, 4 - step)]

    def src_of(step, d):
        dx, dy, dz = d
        if dx:
            return xpk.at[step, (dx + 1) // 2, rows_to(dy)]
        if dy == 0:
            if dz > 0:
                return post[step].at[Z - 1, pl.ds(19 * Y, (10 - step) * Y)]
            return post[step].at[0, pl.ds(step * Y, (10 - step) * Y)]
        if dz == 0:
            return ypk.at[step, (dy + 1) // 2, pl.ds(0, 40 - 2 * step)]
        return ypk.at[step, (dy + 1) // 2, pl.ds(0 if dz > 0 else 4, 4 - step)]

    def message(step, d):
        i = DIRS.index(d)
        return pltpu.make_async_remote_copy(
            src_ref=src_of(step, d), dst_ref=dst_of(step, d),
            send_sem=send_sem.at[step, i], recv_sem=recv_sem.at[step, i],
            device_id=neighbour(d), device_id_type=pl.DeviceIdType.MESH,
        )

    def each(step, chosen, what):
        order = FAR_FIRST if what == "start" else FAR_FIRST[::-1]
        for dz in (0, -1, 1) if what == "start" else (-1, 1, 0):
            dirs = [d for d in order if d in chosen and d[2] == dz]
            if dirs:
                def body(dirs=dirs):
                    for d in dirs:
                        getattr(message(step, d), what)()
                along_z(-dz if what == "wait_recv" else dz, body)

    z_dirs = [d for d in DIRS if d[0] == 0 and d[1] == 0]
    y_dirs = [d for d in DIRS if d[0] == 0 and d[1] != 0]
    x_dirs = [d for d in DIRS if d[0] != 0]

    def put(step, z, values):
        for q in range(27):
            post[step][z, (q + 1) * Y:(q + 2) * Y, :] = values[q]

    def pack(step, packed, z, values, solid):
        for side in (-1, 1):
            acc = packed[side]
            for cy in SIDES:
                for cz in SIDES:
                    col = lane_of(cy, cz, z)
                    shift = (col - (X - 1 if side > 0 else 0)) % X
                    acc = jnp.where(lane == col, pltpu.roll(values[num(side, cy, cz)], shift, 1), acc)
            if step == 0:
                col = 36 + z
                shift = (col - (X - 1 if side > 0 else 0)) % X
                acc = jnp.where(lane == col, pltpu.roll(solid, shift, 1), acc)
            packed[side] = acc
        for side in (-1, 1):
            own = Y - 1 if side > 0 else 0
            for cz in SIDES:
                start = Y_ROW[cz, z]
                first = (num(-1, side, cz) + 1) * Y + own
                ypk[step, (side + 1) // 2, start:start + 3, :] = post[step][
                    z, pl.ds(first, 3, stride=Y), :
                ]
            if step == 0:
                at = Y_SOLID[z]
                ypk[step, (side + 1) // 2, at:at + 1, :] = post[step][z, own:own + 1, :]

    def exchange(step, plane):
        packed = {side: jnp.zeros((Y, X), F32) for side in (-1, 1)}
        for z in (0, 3, 1, 2):
            values = collide(plane(z), target_ref[z], sponge)
            put(step, z, values)
            solid = None
            if step == 0:
                solid = solid_ref[z].astype(F32)
                post[step][z, 0:Y, :] = solid
                own_ref[z] = solid
                post[step][z, 28 * Y:29 * Y, :] = solid
            pack(step, packed, z, values, solid)
            if z == 3 and step == 1:
                each(step, z_dirs, "start")
        for side in (-1, 1):
            xpk[step, (side + 1) // 2] = packed[side]
        if step == 0:
            pl.semaphore_wait(barrier, jnp.where(at_top | at_bottom, 17, 26))
        each(step, x_dirs, "start")
        if step == 0:
            each(step, z_dirs, "start")
        each(step, y_dirs, "start")
        each(step, y_dirs, "wait_recv")
        each(step, z_dirs, "wait_recv")
        if step == 0:
            early_masks[0]()
        for z in range(Z):
            early[step](z)
        if step == 1:
            for sent in range(2):
                for dirs in (z_dirs, y_dirs, x_dirs):
                    each(sent, dirs, "wait_send")
        each(step, x_dirs, "wait_recv")

    def first_plane(z):
        loads[z].wait()
        return [fin[z, q] for q in range(27)]

    for copy in small:
        copy.wait()
    which = row * 0
    for y in range(Y):
        which = jnp.where(row == y, index_ref[y], which)
    for z in range(Z):
        target = jnp.zeros((Y, X), F32)
        for p in range(table_ref.shape[1]):
            entry = jnp.broadcast_to(table_ref[z:z + 1, p:p + 1], (Y, X))
            target = jnp.where(which == p, entry, target)
        target_ref[z] = target
    columns, early_masks, late_masks, early, late = zip(*(
        streaming(
            step, (pre0, pre1)[step], post[step], zr[step], yr[step], er[step], xr[step],
            masks, own_ref, at_top, at_bottom,
        )
        for step in range(2)
    ))
    exchange(0, first_plane)
    cols = columns[0]()
    late_masks[0](cols)
    exchange(1, lambda z: late[0](z, cols))


def last(nz, pre, post, zr, yr, er, xr, masks, own_ref, out_hbm, buf, sem):
    gz = lax.axis_index("gz")
    columns, _, _, _, late = streaming(
        1, pre, post, zr, yr, er, xr, masks, own_ref, gz == nz - 1, gz == 0
    )
    cols = columns()
    copies = []
    for z in range(Z):
        values = late(z, cols)
        for q in range(27):
            buf[z, q] = values[q]
        copies.append(pltpu.make_async_copy(buf.at[z], out_hbm.at[:, z], sem.at[z]))
        copies[-1].start()
    for copy in copies:
        copy.wait()


def shards(mesh_shape, pops, solid, profile_table, profile_index):
    vmem = pl.BlockSpec(memory_space=pltpu.VMEM)
    step_shapes = [(Z, 27, Y, X), (Z, 29 * Y, X), (2, 10 * Y, X), (2, 40, X), (4, Y, X), (26, Y, X)]
    kept_shapes = step_shapes + [(9 * (Z + 2), Y, X), (Z, Y, X)]
    kept = pl.pallas_call(
        functools.partial(kernel, mesh_shape),
        out_shape=[jax.ShapeDtypeStruct(shape, F32) for shape in kept_shapes],
        in_specs=[pl.BlockSpec(memory_space=pltpu.HBM)] * 4,
        out_specs=[vmem] * len(kept_shapes),
        scratch_shapes=[
            pltpu.VMEM((Z, 27, Y, X), F32),
            pltpu.VMEM((Z, Y, X), jnp.int32),
            pltpu.VMEM((Z, profile_table.shape[0]), F32),
            pltpu.SMEM((Y,), jnp.int32),
            pltpu.VMEM((Z, Y, X), F32),
            *[pltpu.VMEM(shape, F32) for shape in step_shapes],
            pltpu.VMEM((2, 2, Y, X), F32),
            pltpu.VMEM((2, 2, 40, X), F32),
            pltpu.SemaphoreType.DMA((Z + 3,)),
            pltpu.SemaphoreType.DMA((2, 26)),
            pltpu.SemaphoreType.DMA((2, 26)),
        ],
        compiler_params=pltpu.CompilerParams(
            collective_id=0, has_side_effects=True, vmem_limit_bytes=32 * 1024 * 1024
        ),
    )(*[
        pltpu.with_memory_space_constraint(a, pltpu.HBM)
        for a in (pops, solid, profile_table.T, profile_index)
    ])
    return pl.pallas_call(
        functools.partial(last, mesh_shape[2]),
        out_shape=jax.ShapeDtypeStruct(pops.shape, F32),
        in_specs=[vmem] * len(kept_shapes),
        out_specs=pl.BlockSpec(memory_space=pl.ANY),
        scratch_shapes=[pltpu.VMEM((Z, 27, Y, X), F32), pltpu.SemaphoreType.DMA((Z,))],
        compiler_params=pltpu.CompilerParams(vmem_limit_bytes=32 * 1024 * 1024),
    )(*kept)


def solution(mesh):
    sizes = tuple(mesh.shape[axis] for axis in ("gx", "gy", "gz"))
    return jax.shard_map(
        functools.partial(shards, sizes),
        mesh=mesh,
        in_specs=(P(None, "gz", "gy", "gx"), P("gz", "gy", "gx"), P(None, "gz"), P("gy")),
        out_specs=P(None, "gz", "gy", "gx"),
        check_vma=False,
    )
```
